256 devices in a mesh: blk: 64 (over x_lo, y, z), tower: 4 (over x_hi, core).
Axes of the slice: x: 4 (x_hi: 2, x_lo: 2; x = x_hi * 2 + x_lo), y: 4, z: 8, core: 2. Of those that a mesh axis runs over, the one named last changes fastest.
Arguments:
- layer_input: bfloat16 [131072, 1152], P(('blk', 'tower')), may hold values from -8 to 8
- caption_ids: int32 [512, 64], P('blk'), may hold values from 0 to 31999, as said below
- positives: int32 [384], P('blk'), may hold values from 0 to 511, as said below
- ln_gain: float32 [2, 1152], replicated, may hold values from 0.1 to 1.9
- w_first: bfloat16 [2, 1152, 2176], P(None, None, 'blk'), may hold values from -0.1875 to 0.1875
- w_second: bfloat16 [2, 2176, 1152], P(None, 'blk'), may hold values from -0.125 to 0.125
- logit_scale: float32 [1], replicated, may hold values from 20 to 80
- logit_bias: float32 [1], replicated, may hold values from -6 to -2
Outputs:
- input_grad: float32 [131072, 1152], P(('blk', 'tower'))
The draws below stay inside these ranges and needn't reach their ends.
Inputs may be any that keep to these rules, and one draw needn't show every extreme that they name: `caption_ids`: each caption's ids are nonzero for its first 32 or more positions and zero after; some caption has no zeros. `positives`: no two images have the same positive caption.
All inputs are finite; a program needn't handle non-finite values.
Results may differ from the reference program's by a relative error of at most 0.013.
Values may be sent and summed in bfloat16 or wider, within the bound.
A program may use at most 128 MiB of HBM per device.

```python
import math
import jax
import jax.numpy as jnp
from jax import lax

D = 1152
PATCHES = 256
TEXT_LEN = 64
VOCAB = 32000
FFW = 2176
IMG_DEV = 2
ROWS = 512
CAP_DEV = 8
IMAGES = 384
CAPTIONS = 512
N_BLK = 64
N_TOWER = 4


def pairing(key):
    return jax.random.permutation(key, CAPTIONS)


def draw_positives(key, part):
    chosen = pairing(key)
    return chosen[:IMAGES].astype(jnp.int32)


def draw_caption_ids(key, part):
    key = jax.random.fold_in(key, 23)
    key_len, key_tok = jax.random.split(key)
    lengths = jax.random.randint(key_len, (CAPTIONS,), TEXT_LEN // 2, TEXT_LEN + 1)
    lengths = lengths.at[0].set(TEXT_LEN)
    tokens = jax.random.randint(key_tok, (CAPTIONS, TEXT_LEN), 1, VOCAB)
    position = jnp.arange(TEXT_LEN)[None, :]
    return jnp.where(position < lengths[:, None], tokens, 0).astype(jnp.int32)


def draw_layer_input(key, part):
    chosen = pairing(key)[:IMAGES]
    key = jax.random.fold_in(key, 31)
    key_cap, key_img, key_noise = jax.random.split(key, 3)
    caption_dir = jax.random.normal(key_cap, (CAPTIONS, D), jnp.float32)
    own_dir = jax.random.normal(key_img, (IMAGES, D), jnp.float32)
    share = 0.25
    noise = jax.random.normal(key_noise, (N_BLK, N_TOWER, ROWS, D), jnp.float32)
    image_offset = share * caption_dir[chosen] + math.sqrt(1.0 - share * share) * own_dir
    image_part = jnp.broadcast_to(image_offset.reshape(N_BLK, N_TOWER - 1, IMG_DEV, 1, D), (N_BLK, N_TOWER - 1, IMG_DEV, PATCHES, D))
    image_part = image_part.reshape(N_BLK, N_TOWER - 1, ROWS, D)
    text_part = jnp.broadcast_to(caption_dir.reshape(N_BLK, 1, CAP_DEV, 1, D), (N_BLK, 1, CAP_DEV, TEXT_LEN, D))
    text_part = text_part.reshape(N_BLK, 1, ROWS, D)
    offsets = jnp.concatenate([image_part, text_part], axis=1)
    values = jnp.clip(offsets + noise, -8.0, 8.0)
    return values.reshape(N_BLK * N_TOWER * ROWS, D).astype(jnp.bfloat16)


def levels(rng, shape, shards, least, largest):
    def one(dim, shards_of):
        heights = jax.random.uniform(jax.random.fold_in(jax.random.fold_in(rng, 6), dim), (shards_of,), jnp.float32, least / len(shards), largest / len(shards))
        return jnp.repeat(jnp.exp(heights), shape[dim] // shards_of).reshape((-1,) + (1,) * (len(shape) - dim - 1))

    level = one(*shards[0])
    for cut in shards[1:]:
        level = level * one(*cut)
    return level


def normal_values(rng, extent, width, most, shards=(), held_as=jnp.bfloat16):
    level = levels(rng, extent, shards, -0.22, 0.18) if shards else 1.0
    result = jax.random.normal(rng, extent, jnp.float32) * width * level
    return jnp.minimum(jnp.maximum(result, -most), most).astype(held_as)


def setup_inputs(seed: int = 0) -> dict:
    arg_keys = jax.random.split(jax.random.key(seed), 9)
    return {
        "layer_input": draw_layer_input(jax.random.fold_in(arg_keys[8], 71), 0),
        "caption_ids": draw_caption_ids(jax.random.fold_in(arg_keys[8], 71), 0),
        "positives": draw_positives(jax.random.fold_in(arg_keys[8], 71), 0),
        "ln_gain": jnp.clip(1.0 + 0.18 * jax.random.normal(arg_keys[3], (2, D), jnp.float32), 0.1, 1.9),
        "w_first": normal_values(arg_keys[4], (2, D, FFW), D ** -0.5, 0.1875, ((2, 64),)),
        "w_second": normal_values(arg_keys[5], (2, FFW, D), FFW ** -0.5, 0.125, ((1, 64),)),
        "logit_scale": jnp.clip(jnp.exp(jax.random.uniform(arg_keys[6], (1,), jnp.float32, math.log(20.0), math.log(80.0))), 20.0, 80.0),
        "logit_bias": jnp.clip(jax.random.uniform(arg_keys[7], (1,), jnp.float32, -6.0, -2.0), -6.0, -2.0),
    }


norm_eps = 1e-06
loss_scale = 128.0
gelu_coeff = 0.7978845608028654

def gelu_pair(pre):
    inner = gelu_coeff * (pre + 0.044715 * pre * pre * pre)
    tanh_part = jnp.tanh(inner)
    value = 0.5 * pre * (1.0 + tanh_part)
    slope = 0.5 * (1.0 + tanh_part) + 0.5 * pre * (1.0 - tanh_part * tanh_part) * gelu_coeff * (1.0 + 3.0 * 0.044715 * pre * pre)
    return (value, slope)

def normalize_rows(rows, gain):
    values = rows.astype(jnp.float32)
    centered = values - lax.optimization_barrier(jnp.mean(values, axis=-1, keepdims=True))
    variance = lax.optimization_barrier(jnp.mean(centered * centered, axis=-1, keepdims=True))
    inv_std = lax.rsqrt(variance + norm_eps)
    standard = centered * inv_std
    normed = (standard * gain).astype(jnp.bfloat16)
    return (values, standard, inv_std, normed)

def block_forward(rows, gain, first, second):
    values, standard, inv_std, normed = normalize_rows(rows, gain)
    pre = jnp.dot(normed, first, preferred_element_type=jnp.float32)
    value, slope = gelu_pair(pre)
    hidden = value.astype(jnp.bfloat16)
    block_out = values + jnp.dot(hidden, second, preferred_element_type=jnp.float32)
    return (block_out, standard, inv_std, slope)

def block_backward(grad_out, standard, inv_std, slope, gain, first, second):
    grad_rows = grad_out.astype(jnp.bfloat16)
    grad_hidden = jnp.dot(grad_rows, second.T, preferred_element_type=jnp.float32)
    grad_pre = (grad_hidden * slope).astype(jnp.bfloat16)
    grad_normed = jnp.dot(grad_pre, first.T, preferred_element_type=jnp.float32)
    grad_std = grad_normed * gain
    first_mean = lax.optimization_barrier(jnp.mean(grad_std, axis=-1, keepdims=True))
    second_mean = lax.optimization_barrier(jnp.mean(grad_std * standard, axis=-1, keepdims=True))
    return grad_out + inv_std * (grad_std - first_mean - standard * second_mean)

def unit_rows(pooled):
    norm = jnp.sqrt(lax.optimization_barrier(jnp.sum(pooled * pooled, axis=-1, keepdims=True)) + norm_eps)
    return (pooled / norm, norm)

def unit_back(unit, norm, grad_emb):
    return (grad_emb - unit * lax.optimization_barrier(jnp.sum(unit * grad_emb, axis=-1, keepdims=True))) / norm

def pool_image(block_out):
    return lax.optimization_barrier(jnp.mean(block_out.reshape(IMG_DEV, PATCHES, D), axis=1))

def pool_text(block_out, mask):
    counts = lax.optimization_barrier(jnp.sum(mask, axis=1, keepdims=True))
    summed = lax.optimization_barrier(jnp.sum(block_out.reshape(CAP_DEV, TEXT_LEN, D) * mask[:, :, None], axis=1))
    return summed / counts

def spread_image(grad_pooled):
    rows = jnp.broadcast_to(grad_pooled[:, None, :] / PATCHES, (IMG_DEV, PATCHES, D))
    return rows.reshape(ROWS, D)

def spread_text(grad_pooled, mask):
    counts = lax.optimization_barrier(jnp.sum(mask, axis=1, keepdims=True))
    rows = grad_pooled[:, None, :] * (mask / counts)[:, :, None]
    return rows.reshape(ROWS, D)

def reference(layer_input, caption_ids, positives, ln_gain, w_first, w_second, logit_scale, logit_bias):
    blocks = layer_input.reshape(N_BLK, N_TOWER, ROWS, D)
    image_blocks = blocks[:, :N_TOWER - 1].reshape(N_BLK * (N_TOWER - 1), ROWS, D)
    text_blocks = blocks[:, N_TOWER - 1]
    masks = (caption_ids != 0).astype(jnp.float32).reshape(N_BLK, CAP_DEV, TEXT_LEN)

    def image_embed(rows):
        block_out, standard, inv_std, slope = block_forward(rows, ln_gain[0], w_first[0], w_second[0])
        return pool_image(block_out)

    def text_embed(pair):
        rows, mask = pair
        block_out, standard, inv_std, slope = block_forward(rows, ln_gain[1], w_first[1], w_second[1])
        return pool_text(block_out, mask)
    image_pool = lax.map(image_embed, image_blocks).reshape(IMAGES, D)
    text_pool = lax.map(text_embed, (text_blocks, masks)).reshape(CAPTIONS, D)
    image_unit, image_norm = unit_rows(image_pool)
    text_unit, text_norm = unit_rows(text_pool)
    image_emb = image_unit.astype(jnp.bfloat16)
    text_emb = text_unit.astype(jnp.bfloat16)
    scale = logit_scale[0]
    bias = logit_bias[0]
    logits = scale * jnp.dot(image_emb, text_emb.T, preferred_element_type=jnp.float32) + bias
    onehot = (positives[:, None] == jnp.arange(CAPTIONS, dtype=jnp.int32)[None, :]).astype(jnp.float32)
    coef = (loss_scale * (jax.nn.sigmoid(logits) - onehot)).astype(jnp.bfloat16)
    grad_image = scale * jnp.dot(coef, text_emb, preferred_element_type=jnp.float32)
    grad_text = scale * jnp.dot(coef.T, image_emb, preferred_element_type=jnp.float32)
    image_gp = unit_back(image_unit, image_norm, grad_image).reshape(N_BLK * (N_TOWER - 1), IMG_DEV, D)
    text_gp = unit_back(text_unit, text_norm, grad_text).reshape(N_BLK, CAP_DEV, D)

    def image_back(pair):
        rows, grad_pooled = pair
        block_out, standard, inv_std, slope = block_forward(rows, ln_gain[0], w_first[0], w_second[0])
        grad_out = spread_image(grad_pooled)
        return block_backward(grad_out, standard, inv_std, slope, ln_gain[0], w_first[0], w_second[0])

    def text_back(triple):
        rows, grad_pooled, mask = triple
        block_out, standard, inv_std, slope = block_forward(rows, ln_gain[1], w_first[1], w_second[1])
        grad_out = spread_text(grad_pooled, mask)
        return block_backward(grad_out, standard, inv_std, slope, ln_gain[1], w_first[1], w_second[1])
    image_grads = lax.map(image_back, (image_blocks, image_gp)).reshape(N_BLK, N_TOWER - 1, ROWS, D)
    text_grads = lax.map(text_back, (text_blocks, text_gp, masks)).reshape(N_BLK, 1, ROWS, D)
    joined = jnp.concatenate([image_grads, text_grads], axis=1)
    return joined.reshape(N_BLK * N_TOWER * ROWS, D)
```

```python
import functools

import jax
import jax.numpy as jnp
from jax import lax
from jax.experimental import pallas as pl
from jax.experimental.pallas import tpu as pltpu
from jax.sharding import PartitionSpec as P

D = 1152
ROWS = 512
N_Y = 4
N_Z = 8
MAIN = 32
GROUP = N_Z * MAIN
EXTRA = 16
SEG = 64
LANES = 128
KEYED = D + LANES

norm_eps = 1e-06
loss_scale = 128.0
gelu_c = 0.7978845608028654
gelu_k = gelu_c * 0.044715

MESH = pl.DeviceIdType.MESH
bf16 = jnp.bfloat16
f32 = jnp.float32


def dot_nt(left, right):
    return lax.dot_general(left, right, (((1,), (1,)), ((), ())), preferred_element_type=f32)


def dot_nn(left, right):
    return jnp.dot(left, right, preferred_element_type=f32)


def device_of(x, y, z, core):
    x = lax.rem(x + 8, 4)
    y = lax.rem(y + 8, N_Y)
    z = lax.rem(z + 16, N_Z)
    return (lax.rem(x, 2) * (N_Y * N_Z) + y * N_Z + z, (x // 2) * 2 + core)


def normalise(rows):
    values = rows.astype(f32)
    centered = values - jnp.mean(values, axis=-1, keepdims=True)
    variance = jnp.mean(centered * centered, axis=-1, keepdims=True)
    inv_std = lax.rsqrt(variance + norm_eps)
    return centered * inv_std, inv_std


def kernel(
    x_ref, rowmask_ref, pmask_ref, count_ref, key_ref, gain_ref, w1_ref, w2_ref, scale_ref, bias_ref,
    out_ref,
    wa, wb, ea, eb, exa, exb, normed, pre, slope, slope_e, pooled, pooled_e, acc,
    tile, column, bundle, others, part, gsum, gpre,
    recv_main, recv_ex, recv_e, send_zm, send_ze, send_ym, send_ye, send_xm, send_xe,
    c_send, c_recv, o_send, o_recv, g_send, g_recv,
):
    blk = lax.axis_index("blk")
    tower = lax.axis_index("tower")
    x_lo = blk // (N_Y * N_Z)
    y = lax.rem(blk // N_Z, N_Y)
    z = lax.rem(blk, N_Z)
    x_hi = tower // 2
    core = lax.rem(tower, 2)
    x = x_hi * 2 + x_lo
    is_text = tower == 3
    t = jnp.where(is_text, 1, 0)
    role = x * 2 + core
    gid = x_lo * N_Y + y

    toward = jnp.where(core == 1, 1 - 2 * x_lo, 2 * x_lo - 1)
    partner = device_of(x + toward, y, z, core)

    def ring_z(d):
        return device_of(x, y, z + d, core)

    def ring_y(d):
        return device_of(x, y + d, z, core)

    def in_column(d):
        q = lax.rem(role + d, 8)
        return device_of(q // 2, y, z, lax.rem(q, 2))

    barrier = pltpu.get_barrier_semaphore()
    for d in range(1, N_Z):
        pl.semaphore_signal(barrier, inc=1, device_id=ring_z(d), device_id_type=MESH)
    for d in range(1, N_Y):
        pl.semaphore_signal(barrier, inc=1, device_id=ring_y(d), device_id_type=MESH)
    for d in range(1, 8):
        pl.semaphore_signal(barrier, inc=1, device_id=in_column(d), device_id_type=MESH)
    for d in range(1, N_Y):
        pl.semaphore_signal(barrier, inc=1, device_id=device_of(x, y - d, z + role, core), device_id_type=MESH)

    @pl.when(role != 0)
    def _():
        pl.semaphore_signal(barrier, inc=1, device_id=device_of(x, y, z + role, core), device_id_type=MESH)

    row = lax.broadcasted_iota(jnp.int32, (MAIN + EXTRA, 34), 0)
    col = lax.broadcasted_iota(jnp.int32, (MAIN + EXTRA, 34), 1)
    lead = jnp.logical_and(row < MAIN, row == col)
    rest = jnp.logical_and(col >= MAIN, row - 2 * z == col)
    pick = jnp.where(jnp.logical_or(lead, rest), 1.0, 0.0).astype(bf16)
    own = dot_nt(pick, w1_ref[t]).astype(bf16)
    wa[gid, z] = own[:MAIN]
    exa[z] = own[MAIN:]
    own = dot_nn(pick, w2_ref[t]).astype(bf16)
    wb[gid, z] = own[:MAIN]
    exb[z] = own[MAIN:]
    pl.semaphore_wait(barrier, jnp.where(role == 0, 20, 21))

    pending = []

    def send(ref, at, send_sem, recv_sem, target):
        copy = pltpu.make_async_remote_copy(
            src_ref=ref.at[at], dst_ref=ref.at[at], send_sem=send_sem, recv_sem=recv_sem,
            device_id=target, device_id_type=MESH,
        )
        copy.start()
        pending.append(copy)

    def arrived(ref, at, recv_sem):
        pltpu.make_async_remote_copy(
            src_ref=ref.at[at], dst_ref=ref.at[at], send_sem=recv_sem, recv_sem=recv_sem,
            device_id=partner, device_id_type=MESH,
        ).wait_recv()

    mats = ((wa, ea, exa), (wb, eb, exb))
    z_order = (0, 1, 7, 2, 6, 3, 5, 4)
    y_order = (0, 1, 3, 2)

    def zid(d):
        return lax.rem(z + d, N_Z)

    def gid_of(dy, other=0):
        half = 1 - x_lo if other else x_lo
        return half * N_Y + lax.rem(y + dy, N_Y)

    def send_z(m):
        w, e, ex = mats[m]
        for d in z_order[1:]:
            send(w, (gid, z), send_zm.at[m, d - 1], recv_main.at[m, gid, z], ring_z(d))
            send(ex, z, send_ze.at[m, d - 1], recv_ex.at[m, z], ring_z(d))

    def send_x(m, dy, d):
        w = mats[m][0]
        g, zz = gid_of(dy), zid(d)
        send(w, (g, zz), send_xm.at[m, dy, d], recv_main.at[m, g, zz], partner)

    def send_y(m, d):
        w = mats[m][0]
        zz = zid(d)
        for dy in (1, 3, 2):
            send(w, (gid, zz), send_ym.at[m, dy - 1, d], recv_main.at[m, gid, zz], ring_y(dy))

    def take(m, dy, other, d):
        g, zz = gid_of(dy, other), zid(d)
        arrived(mats[m][0], (g, zz), recv_main.at[m, g, zz])

    def extras(m):
        w, e, ex = mats[m]
        for d in range(1, N_Z):
            arrived(ex, zid(d), recv_ex.at[m, zid(d)])
        total = ex[0].astype(f32)
        for k in range(1, N_Z):
            total += ex[k].astype(f32)
        e[gid] = total.astype(bf16)
        for dy in (1, 3, 2):
            send(e, gid, send_ye.at[m, dy - 1], recv_e.at[m, gid], ring_y(dy))
        send(e, gid, send_xe.at[m, 0], recv_e.at[m, gid], partner)

    def extras_x(m, dy):
        w, e, ex = mats[m]
        g = gid_of(dy)
        arrived(e, g, recv_e.at[m, g])
        send(e, g, send_xe.at[m, dy], recv_e.at[m, g], partner)

    gain = gain_ref[pl.ds(t, 1), :]

    def norm_block(j):
        standard, _ = normalise(x_ref[pl.ds(j * SEG, SEG), :])
        normed[pl.ds(j * SEG, SEG), :] = (standard * gain).astype(bf16)

    def activate(width, weights, slope_at, pool_at):
        pre[:, :width] = dot_nt(normed[...], weights)

        def step(k, carry):
            rows = pl.ds(k * SEG, SEG)
            p = pre[rows, :width]
            u = p * p
            h = 0.5 + 0.5 * jnp.tanh(p * (gelu_c + gelu_k * u))
            value = p * h
            hidden[rows, :width] = value.astype(bf16)
            s = h + value * ((1.0 - h) * (2.0 * gelu_c + 6.0 * gelu_k * u))
            slope_at(rows, s * rowmask_ref[rows, :])
            return carry

        lax.fori_loop(0, ROWS // SEG, step, 0)
        pool_at(dot_nn(pmask_ref[...], hidden[:, :width]))

    hidden = gpre

    def group_forward(g):
        def slope_at(rows, s):
            slope[g, rows, :] = s

        def pool_at(v):
            pooled[g] = v

        activate(GROUP, wa[g].reshape(GROUP, D), slope_at, pool_at)

    def pair(v):
        hi = v.astype(bf16)
        lo = (v - hi.astype(f32)).astype(bf16)
        return jnp.concatenate([hi, lo], axis=0)

    def group_out(g):
        acc[...] += dot_nn(pair(pooled[g]), wb[g].reshape(GROUP, D))

    send_z(0)
    send_y(0, 0)
    send_x(0, 0, 0)
    norm_block(0)
    for k, d in enumerate(z_order[1:]):
        norm_block(k + 1)
        take(0, 0, 0, d)
        send_y(0, d)
        send_x(0, 0, d)
    extras(0)
    send_z(1)
    group_forward(gid)
    for dy in y_order[1:]:
        for d in z_order:
            take(0, dy, 0, d)
            send_x(0, dy, d)
        extras_x(0, dy)
        group_forward(gid_of(dy))

    send_y(1, 0)
    send_x(1, 0, 0)
    for d in z_order[1:]:
        take(1, 0, 0, d)
        send_y(1, d)
        send_x(1, 0, d)
    extras(1)
    for dy in y_order:
        for d in z_order:
            take(0, dy, 1, d)
        arrived(ea, gid_of(dy, 1), recv_e.at[0, gid_of(dy, 1)])
        group_forward(gid_of(dy, 1))

    def slope_at_e(rows, s):
        slope_e[rows, :] = s

    def pool_at_e(v):
        pooled_e[...] = v

    activate(LANES, ea[...].reshape(LANES, D), slope_at_e, pool_at_e)
    sums = dot_nn(pmask_ref[...], x_ref[...])
    acc[...] = jnp.zeros_like(acc)
    group_out(gid)
    for dy in y_order[1:]:
        for d in z_order:
            take(1, dy, 0, d)
            send_x(1, dy, d)
        extras_x(1, dy)
        group_out(gid_of(dy))
    for dy in y_order:
        for d in z_order:
            take(1, dy, 1, d)
        arrived(eb, gid_of(dy, 1), recv_e.at[1, gid_of(dy, 1)])
        group_out(gid_of(dy, 1))
    acc[...] += dot_nn(pair(pooled_e[...]), eb[...].reshape(LANES, D))
    sums = sums + acc[0:8, :] + acc[8:16, :]

    seg = lax.broadcasted_iota(jnp.int32, (8, D), 0)
    first = jnp.sum(sums[0:4], axis=0, keepdims=True)
    second = jnp.sum(sums[4:8], axis=0, keepdims=True)
    sums = jnp.where(is_text, sums, jnp.where(seg < 4, first, second))
    count = count_ref[...]
    value = sums / count
    norm = jnp.sqrt(jnp.sum(value * value, axis=-1, keepdims=True) + norm_eps)
    unit = value / norm

    at16 = lax.broadcasted_iota(jnp.int32, (16, D), 0)
    lead_row = x_lo * 6 + tower * 2
    zero8 = jnp.zeros((8, D), f32)
    low = jnp.where(x_lo == 0, unit, zero8)
    high = jnp.where(x_lo == 0, zero8, unit)
    text_tile = jnp.concatenate([low, high], axis=0)
    image_tile = jnp.where(at16 == lead_row, unit[0:1], jnp.where(at16 == lead_row + 1, unit[4:5], 0.0))
    tile[:, :D] = jnp.where(is_text, text_tile, image_tile).astype(bf16)
    tile[:, D:] = key_ref[...]
    for d in range(1, 8):
        copy = pltpu.make_async_remote_copy(
            src_ref=tile, dst_ref=column.at[role], send_sem=c_send.at[d - 1], recv_sem=c_recv.at[role],
            device_id=in_column(d), device_id_type=MESH,
        )
        copy.start()
        pending.append(copy)
    column[role] = tile[...]
    for d in range(1, 8):
        q = lax.rem(role + d, 8)
        arrived(column, q, c_recv.at[q])
    bundle[0:16, :] = column[5] + column[7]
    images = column[0]
    for q in (1, 2, 3, 4, 6):
        images = images + column[q]
    bundle[16:32, :] = images

    for d in range(1, N_Y):
        copy = pltpu.make_async_remote_copy(
            src_ref=bundle, dst_ref=others.at[d], send_sem=o_send.at[d], recv_sem=o_recv.at[d],
            device_id=device_of(x, y + d, z - role, core), device_id_type=MESH,
        )
        copy.start()
        pending.append(copy)

    def straight():
        return pltpu.make_async_remote_copy(
            src_ref=bundle, dst_ref=others.at[0], send_sem=o_send.at[0], recv_sem=o_recv.at[0],
            device_id=device_of(x, y, z - role, core), device_id_type=MESH,
        )

    @pl.when(role != 0)
    def _():
        copy = straight()
        copy.start()
        copy.wait()

    @pl.when(role == 0)
    def _():
        others[0] = bundle[...]

    for d in range(1, N_Y):
        arrived(others, d, o_recv.at[d])

    scale = scale_ref[0]
    bias = bias_ref[0]
    far = others[...].reshape(N_Y * 32, KEYED)
    logits = scale * dot_nt(bundle[:, :D], far[:, :D]) + bias
    lane = lax.broadcasted_iota(jnp.int32, (32, LANES), 1)
    place = lax.broadcasted_iota(jnp.int32, (32, LANES), 0)
    base = jnp.where(lane == 0, 16.0, jnp.where(lane == 1, 1.0, 0.0)).astype(bf16)
    key_col = dot_nt(base, far[:, D:])
    key_row = dot_nt(bundle[:, D:], jnp.concatenate([base] * 4, axis=0))
    lane32 = lax.rem(lane, 32)
    row_text, col_text = place < 16, lane32 < 16
    row_image = jnp.logical_and(place >= 16, place < 28)
    col_image = jnp.logical_and(lane32 >= 16, lane32 < 28)
    cross = jnp.logical_or(
        jnp.logical_and(row_text, col_image), jnp.logical_and(row_image, col_text)
    )
    match = jnp.where(key_col == key_row, 1.0, 0.0)
    coef = jnp.where(cross, loss_scale * (jax.nn.sigmoid(logits) - match), 0.0).astype(bf16)
    part[...] = (scale * dot_nn(coef, far[:, :D])).reshape(4, 8, D)

    def rows_of(q):
        qx = q // 2
        qlo = lax.rem(qx, 2)
        group = (qx // 2) * 2 + lax.rem(q, 2)
        return jnp.where(group == 3, qlo, 2 + (qlo * 6 + group * 2) // 8)

    for d in range(1, 8):
        q = lax.rem(role + d, 8)
        copy = pltpu.make_async_remote_copy(
            src_ref=part.at[rows_of(q)], dst_ref=gsum.at[role], send_sem=g_send.at[d - 1],
            recv_sem=g_recv.at[role], device_id=in_column(d), device_id_type=MESH,
        )
        copy.start()
        pending.append(copy)
    gsum[role] = part[rows_of(role)]
    for d in range(1, 8):
        q = lax.rem(role + d, 8)
        arrived(gsum, q, g_recv.at[q])
    grad = gsum[0]
    for q in range(1, 8):
        grad = grad + gsum[q]
    mine = lax.rem(lead_row, 8)
    g0 = jnp.sum(jnp.where(seg == mine, grad, 0.0), axis=0, keepdims=True)
    g1 = jnp.sum(jnp.where(seg == mine + 1, grad, 0.0), axis=0, keepdims=True)
    grad = jnp.where(is_text, grad, jnp.where(seg < 4, g0, g1))
    grad = (grad - unit * jnp.sum(unit * grad, axis=-1, keepdims=True)) / norm
    grad = grad / count
    grad_rows = grad.astype(bf16)

    def back(width, weights, slope_of, at):
        gh = dot_nt(grad_rows, weights)
        for j in range(8):
            rows = slice(j * SEG, (j + 1) * SEG)
            gpre[rows, at : at + width] = (slope_of(rows) * gh[j : j + 1, :]).astype(bf16)

    for g in range(8):
        back(GROUP, wb[g].reshape(GROUP, D), lambda rows, g=g: slope[g, rows, :], g * GROUP)
    back(LANES, eb[...].reshape(LANES, D), lambda rows: slope_e[rows, :], 8 * GROUP)
    out_ref[...] = dot_nn(gpre[:, : 8 * GROUP], wa[...].reshape(8 * GROUP, D)) + dot_nn(
        gpre[:, 8 * GROUP :], ea[...].reshape(LANES, D)
    )
    for j in range(8):
        rows = slice(j * SEG, (j + 1) * SEG)
        standard, inv_std = normalise(x_ref[rows, :])
        grad_std = out_ref[rows, :] * gain
        m1 = jnp.mean(grad_std, axis=-1, keepdims=True)
        m2 = jnp.mean(grad_std * standard, axis=-1, keepdims=True)
        out_ref[rows, :] = grad[j : j + 1, :] * rowmask_ref[rows, :] + inv_std * (
            grad_std - m1 - standard * m2
        )
    for copy in pending:
        copy.wait_send()


def body(layer_input, caption_ids, positives, ln_gain, w_first, w_second, logit_scale, logit_bias):
    tower = lax.axis_index("tower")
    blk = lax.axis_index("blk")
    x_lo = blk // (N_Y * N_Z)
    is_text = tower == 3
    mask = jnp.where(is_text, caption_ids != 0, True)
    rowmask = mask.astype(f32).reshape(ROWS, 1)
    same = jnp.arange(ROWS)[None, :] // SEG == jnp.arange(8)[:, None]
    pmask = jnp.where(same, mask.reshape(1, ROWS), False).astype(bf16)
    count = jnp.where(is_text, jnp.sum(mask.astype(f32), axis=1, keepdims=True), 256.0)
    r = jnp.arange(16)
    text_key = 8 * blk + r - 8 * x_lo
    rel = r - (x_lo * 6 + tower * 2)
    two = lax.dynamic_slice_in_dim(positives, 2 * jnp.minimum(tower, 2), 2, 0)
    image_key = jnp.where(rel == 0, two[0], two[1])
    in_text = jnp.logical_and(r >= 8 * x_lo, r < 8 * x_lo + 8)
    in_image = jnp.logical_and(rel >= 0, rel < 2)
    key = jnp.where(is_text, jnp.where(in_text, text_key, 0), jnp.where(in_image, image_key, 0))
    lane = jnp.arange(LANES)[None, :]
    key_tile = jnp.where(lane == 0, (key // 16)[:, None], jnp.where(lane == 1, (key % 16)[:, None], 0))
    key_tile = key_tile.astype(f32).astype(bf16)

    vmem = pl.BlockSpec(memory_space=pltpu.VMEM)
    smem = pl.BlockSpec(memory_space=pltpu.SMEM)
    dma = pltpu.SemaphoreType.DMA
    return pl.pallas_call(
        kernel,
        out_shape=jax.ShapeDtypeStruct((ROWS, D), f32),
        in_specs=[vmem] * 8 + [smem] * 2,
        out_specs=vmem,
        scratch_shapes=[
            pltpu.VMEM((8, N_Z, MAIN, D), bf16),
            pltpu.VMEM((8, N_Z, MAIN, D), bf16),
            pltpu.VMEM((8, EXTRA, D), bf16),
            pltpu.VMEM((8, EXTRA, D), bf16),
            pltpu.VMEM((N_Z, EXTRA, D), bf16),
            pltpu.VMEM((N_Z, EXTRA, D), bf16),
            pltpu.VMEM((ROWS, D), bf16),
            pltpu.VMEM((ROWS, GROUP), f32),
            pltpu.VMEM((8, ROWS, GROUP), f32),
            pltpu.VMEM((ROWS, LANES), f32),
            pltpu.VMEM((8, 8, GROUP), f32),
            pltpu.VMEM((8, LANES), f32),
            pltpu.VMEM((16, D), f32),
            pltpu.VMEM((16, KEYED), bf16),
            pltpu.VMEM((8, 16, KEYED), bf16),
            pltpu.VMEM((32, KEYED), bf16),
            pltpu.VMEM((N_Y, 32, KEYED), bf16),
            pltpu.VMEM((4, 8, D), f32),
            pltpu.VMEM((8, 8, D), f32),
            pltpu.VMEM((ROWS, 8 * GROUP + LANES), bf16),
            dma((2, 8, 8)),
            dma((2, 8)),
            dma((2, 8)),
            dma((2, 7)),
            dma((2, 7)),
            dma((2, 3, 8)),
            dma((2, 3)),
            dma((2, 4, 8)),
            dma((2, 4)),
            dma((7,)),
            dma((8,)),
            dma((4,)),
            dma((4,)),
            dma((7,)),
            dma((8,)),
        ],
        compiler_params=pltpu.CompilerParams(
            collective_id=0, has_side_effects=True, vmem_limit_bytes=56 * 2**20
        ),
        name="step",
    )(
        layer_input, rowmask, pmask, count, key_tile, ln_gain, w_first, w_second,
        logit_scale, logit_bias,
    )


def solution(mesh):
    placed = (
        P(("blk", "tower"), None),
        P("blk", None),
        P("blk"),
        P(),
        P(None, None, "blk"),
        P(None, "blk", None),
        P(),
        P(),
    )
    return jax.shard_map(
        body, mesh=mesh, in_specs=placed, out_specs=P(("blk", "tower"), None), check_vma=False
    )
```

```python
import functools

import jax
import jax.numpy as jnp
from jax import lax
from jax.experimental import pallas as pl
from jax.experimental.pallas import tpu as pltpu
from jax.sharding import PartitionSpec as P

D = 1152
ROWS = 512
N_Y = 4
N_Z = 8
MAIN = 32
GROUP = N_Z * MAIN
EXTRA = 16
SEG = 64
LANES = 128
KEYED = D + LANES
FRONT = 896
SECOND = 14.0

norm_eps = 1e-06
loss_scale = 128.0
gelu_c = 0.7978845608028654
gelu_k = gelu_c * 0.044715

MESH = pl.DeviceIdType.MESH
bf16 = jnp.bfloat16
f32 = jnp.float32


def dot_nt(left, right):
    return lax.dot_general(left, right, (((1,), (1,)), ((), ())), preferred_element_type=f32)


def dot_nn(left, right):
    return jnp.dot(left, right, preferred_element_type=f32)


def device_of(x, y, z, core):
    x = lax.rem(x + 8, 4)
    y = lax.rem(y + 8, N_Y)
    z = lax.rem(z + 16, N_Z)
    return (lax.rem(x, 2) * (N_Y * N_Z) + y * N_Z + z, (x // 2) * 2 + core)


def normalise(rows):
    values = rows.astype(f32)
    centered = values - jnp.mean(values, axis=-1, keepdims=True)
    variance = jnp.mean(centered * centered, axis=-1, keepdims=True)
    inv_std = lax.rsqrt(variance + norm_eps)
    return centered * inv_std, inv_std


def kernel(
    x_ref, ids_ref, gain_ref, w1_ref, w2_ref, positive_ref, scale_ref, bias_ref,
    out_ref,
    wa, wb, ea, eb, exa, exb, normed, pre, slope, slope_e, pooled, pooled_e, acc,
    pmask, rowmask, tile_t, tile_i, column_t, column_i, bundle, others,
    part_t, part_i, gsum_t, gsum_i, grad_at, gpre,
    recv_main, recv_by, recv_bx, recv_bz, send_by, send_bx, send_bl, send_bs, recv_ex, recv_e, send_zm, send_ze, send_ym, send_ye, send_xm, send_xe,
    c_send, c_recv, o_send, o_recv, g_send, g_recv,
):
    blk = lax.axis_index("blk")
    tower = lax.axis_index("tower")
    x_lo = blk // (N_Y * N_Z)
    y = lax.rem(blk // N_Z, N_Y)
    z = lax.rem(blk, N_Z)
    x_hi = tower // 2
    core = lax.rem(tower, 2)
    x = x_hi * 2 + x_lo
    is_text = tower == 3
    t = jnp.where(is_text, 1, 0)
    role = x * 2 + core
    gid = x_lo * N_Y + y

    def far_at(k):
        side = 1 - 2 * core
        odd = lax.rem(x, 2)
        dy = jnp.where(odd == 1, 2 * (k // 2) + x // 2, k)
        dz = jnp.where(odd == 1, side * (1 + 2 * (k % 2)), jnp.where(x == 0, 4 * core, 2 * side))
        return dy, dz

    def far_from(k):
        dy, dz = far_at(k)
        return device_of(x, y - dy, z + dz, core)

    def far_to(k):
        dy, dz = far_at(k)
        return device_of(x, y + dy, z - dz, core)

    toward = jnp.where(core == 1, 1 - 2 * x_lo, 2 * x_lo - 1)
    partner = device_of(x + toward, y, z, core)

    def ring_z(d):
        return device_of(x, y, z + d, core)

    def ring_y(d):
        return device_of(x, y + d, z, core)

    def in_column(d):
        q = lax.rem(role + d, 8)
        return device_of(q // 2, y, z, lax.rem(q, 2))

    barrier = pltpu.get_barrier_semaphore()
    for d in range(1, N_Z):
        pl.semaphore_signal(barrier, inc=1, device_id=ring_z(d), device_id_type=MESH)
    for d in range(1, N_Y):
        pl.semaphore_signal(barrier, inc=1, device_id=ring_y(d), device_id_type=MESH)
    for d in range(1, 8):
        pl.semaphore_signal(barrier, inc=1, device_id=in_column(d), device_id_type=MESH)
    for k in range(1, N_Y):
        pl.semaphore_signal(barrier, inc=1, device_id=far_from(k), device_id_type=MESH)

    @pl.when(role != 0)
    def _():
        pl.semaphore_signal(barrier, inc=1, device_id=far_from(0), device_id_type=MESH)

    row = lax.broadcasted_iota(jnp.int32, (MAIN + EXTRA, 68), 0)
    col = lax.broadcasted_iota(jnp.int32, (MAIN + EXTRA, 68), 1)
    lead = jnp.logical_and(row < MAIN, 2 * row + t == col)
    rest = jnp.logical_and(col >= 2 * MAIN, 2 * (row - 2 * z) + t == col)
    pick = jnp.where(jnp.logical_or(lead, rest), 1.0, 0.0).astype(bf16)
    for ref, w, ex in ((w1_ref, wa, exa), (w2_ref, wb, exb)):
        own = dot_nn(pick, ref[...].reshape(68, D)).astype(bf16)
        w[gid, z] = own[:MAIN]
        ex[0] = own[MAIN:]

    mask = jnp.where(is_text, jnp.where(ids_ref[...] != 0, 1.0, 0.0), 1.0)
    count = jnp.where(is_text, jnp.sum(mask, axis=1, keepdims=True), 256.0)
    slot = lax.broadcasted_iota(jnp.int32, (SEG, ROWS), 0)
    at = lax.broadcasted_iota(jnp.int32, (SEG, ROWS), 1)
    spread = jnp.where(lax.rem(at, SEG) == slot, 1.0, 0.0).astype(bf16)
    wide = dot_nn(mask.astype(bf16), spread)
    segment = lax.broadcasted_iota(jnp.int32, (8, ROWS), 0)
    at = lax.broadcasted_iota(jnp.int32, (8, ROWS), 1)
    pmask[...] = jnp.where(at // SEG == segment, wide, 0.0).astype(bf16)
    rowmask[...] = lax.dot_general(
        pmask[...], jnp.ones((8, LANES), bf16), (((0,), (0,)), ((), ())), preferred_element_type=f32
    )

    def mask_of(rows, width):
        return jnp.concatenate([rowmask[rows, :]] * (width // LANES), axis=1)

    pl.semaphore_wait(barrier, jnp.where(role == 0, 20, 21))

    pending = []

    def send(ref, at, send_sem, recv_sem, target):
        copy = pltpu.make_async_remote_copy(
            src_ref=ref.at[at], dst_ref=ref.at[at], send_sem=send_sem, recv_sem=recv_sem,
            device_id=target, device_id_type=MESH,
        )
        copy.start()
        pending.append(copy)

    def arrived(ref, at, recv_sem):
        pltpu.make_async_remote_copy(
            src_ref=ref.at[at], dst_ref=ref.at[at], send_sem=recv_sem, recv_sem=recv_sem,
            device_id=partner, device_id_type=MESH,
        ).wait_recv()

    mats = ((wa, ea, exa), (wb, eb, exb))
    z_order = (0, 1, 7, 2, 6, 3, 5, 4)
    y_order = (0, 1, 3, 2)

    def zid(d):
        return lax.rem(z + d, N_Z)

    def gid_of(dy, other=0):
        half = 1 - x_lo if other else x_lo
        return half * N_Y + lax.rem(y + dy, N_Y)

    front = pl.ds(0, FRONT)
    back_cols = pl.ds(FRONT, D - FRONT)
    every = pl.ds(0, MAIN)
    long = 1 - 2 * core

    def half_of(other):
        return pl.ds((1 - x_lo if other else x_lo) * N_Y, N_Y)

    def send_z(m):
        for d in z_order[1:]:
            send(mats[m][0], (gid, z, every, front), send_zm.at[m, d - 1], recv_main.at[m, gid, z], ring_z(d))

    def send_x(m, dy, d):
        g, zz = gid_of(dy), zid(d)
        send(mats[m][0], (g, zz, every, front), send_xm.at[m, dy, d], recv_main.at[m, g, zz], partner)

    def send_y(m, d):
        zz = zid(d)
        for dy in (1, 3, 2):
            send(
                mats[m][0], (gid, zz, every, front), send_ym.at[m, dy - 1, d], recv_main.at[m, gid, zz], ring_y(dy)
            )

    def take(m, dy, other, d):
        g, zz = gid_of(dy, other), zid(d)
        arrived(mats[m][0], (g, zz, every, front), recv_main.at[m, g, zz])

    def back_y(m):
        for dy in (1, 3, 2):
            send(mats[m][0], (gid, z, every, back_cols), send_by.at[m, dy - 1], recv_by.at[m, y], ring_y(dy))

    def back_ring(m, other, hop):
        at = lambda zz: (half_of(other), zz, every, back_cols)
        h = 1 if other else 0
        w = mats[m][0]
        there = lax.rem(z - long * hop + 2 * N_Z, N_Z)
        here = lax.rem(z + long * hop + 2 * N_Z, N_Z)
        half = 1 - x_lo if other else x_lo
        if 0 < hop:
            arrived(w, at(there), recv_bz.at[m, half, there])
            if hop < 4:
                arrived(w, at(here), recv_bz.at[m, half, here])
        if hop < 4:
            send(w, at(there), send_bl.at[m, h, hop], recv_bz.at[m, half, there], ring_z(long))
        if hop < 3:
            send(w, at(here), send_bs.at[m, h, hop], recv_bz.at[m, half, here], ring_z(-long))

    def back_own(m):
        w = mats[m][0]
        for dy in (1, 3, 2):
            yy = lax.rem(y + dy, N_Y)
            arrived(w, (gid_of(dy), z, every, back_cols), recv_by.at[m, yy])
        send(w, (half_of(0), z, every, back_cols), send_bx.at[m], recv_bx.at[m], partner)
        back_ring(m, 0, 0)

    def back_partner(m):
        arrived(mats[m][0], (half_of(1), z, every, back_cols), recv_bx.at[m])
        back_ring(m, 1, 0)

    def extras_send(m, k):
        w, e, ex = mats[m]
        bit = 1 << k
        other = z + bit - 2 * bit * lax.rem(z // bit, 2)
        copy = pltpu.make_async_remote_copy(
            src_ref=ex.at[2 * k], dst_ref=ex.at[2 * k + 1], send_sem=send_ze.at[m, k],
            recv_sem=recv_ex.at[m, k], device_id=device_of(x, y, other, core), device_id_type=MESH,
        )
        copy.start()
        pending.append(copy)

    def extras_take(m, k):
        w, e, ex = mats[m]
        arrived(ex, 2 * k + 1, recv_ex.at[m, k])
        total = (ex[2 * k].astype(f32) + ex[2 * k + 1].astype(f32)).astype(bf16)
        if k < 2:
            ex[2 * k + 2] = total
            extras_send(m, k + 1)
            return
        e[gid] = total
        for dy in (1, 3, 2):
            send(e, gid, send_ye.at[m, dy - 1], recv_e.at[m, gid], ring_y(dy))
        send(e, gid, send_xe.at[m, 0], recv_e.at[m, gid], partner)

    def extras_x(m, dy):
        w, e, ex = mats[m]
        g = gid_of(dy)
        arrived(e, g, recv_e.at[m, g])
        send(e, g, send_xe.at[m, dy], recv_e.at[m, g], partner)

    gain = gain_ref[pl.ds(t, 1), :]

    def norm_block(j):
        standard, _ = normalise(x_ref[pl.ds(j * SEG, SEG), :])
        normed[pl.ds(j * SEG, SEG), :] = (standard * gain).astype(bf16)

    def activate(width, weights, slope_at, pool_at):
        pre[:, :width] = dot_nt(normed[...], weights)

        def step(k, carry):
            rows = pl.ds(k * SEG, SEG)
            p = pre[rows, :width]
            u = p * p
            h = 0.5 + 0.5 * jnp.tanh(p * (gelu_c + gelu_k * u))
            value = p * h
            hidden[rows, :width] = value.astype(bf16)
            s = h + value * ((1.0 - h) * (2.0 * gelu_c + 6.0 * gelu_k * u))
            slope_at(rows, s * mask_of(rows, width))
            return carry

        lax.fori_loop(0, ROWS // SEG, step, 0)
        pool_at(dot_nn(pmask[...], hidden[:, :width]))

    hidden = gpre

    def group_forward(g):
        def slope_at(rows, s):
            slope[g, rows, :] = s

        def pool_at(v):
            pooled[g] = v

        activate(GROUP, wa[g].reshape(GROUP, D), slope_at, pool_at)

    def pair(v):
        hi = v.astype(bf16)
        lo = (v - hi.astype(f32)).astype(bf16)
        return jnp.concatenate([hi, lo], axis=0)

    def group_out(g):
        acc[...] += dot_nn(pair(pooled[g]), wb[g].reshape(GROUP, D))

    def slope_at_e(rows, s):
        slope_e[rows, :] = s

    def pool_at_e(v):
        pooled_e[...] = v

    steps = []

    def due(when, act, *args):
        steps.append((when, len(steps), act, args))

    def start(m):
        send_z(m)
        back_y(m)
        send_y(m, 0)
        send_x(m, 0, 0)
        extras_send(m, 0)

    def z_arrival(m, d):
        take(m, 0, 0, d)
        send_y(m, d)
        send_x(m, 0, d)

    def y_arrival(m, d):
        for dy in y_order[1:]:
            take(m, dy, 0, d)
            send_x(m, dy, d)

    def x_arrival(m, dy):
        for d in z_order:
            take(m, dy, 1, d)

    def extras_rest(m):
        for dy in y_order[1:]:
            extras_x(m, dy)

    def extras_last(m):
        for dy in y_order:
            arrived(mats[m][1], gid_of(dy, 1), recv_e.at[m, gid_of(dy, 1)])

    for j in range(8):
        due(0.1 + 1.0 * j, norm_block, j)
    for m, at in ((0, 0.0), (1, SECOND)):
        due(at, start, m)
        for n, d in enumerate(z_order[1:]):
            due(at + 4.4 + 1.3 * n, z_arrival, m, d)
        for n, d in enumerate(z_order):
            due(at + 7.0 + 2.3 * n, y_arrival, m, d)
        due(at + 5.0, back_own, m)
        due(at + 8.0, back_partner, m)
        for hop in range(1, 5):
            due(at + 6.0 + 4.0 * hop, back_ring, m, 0, hop)
            due(at + 9.0 + 4.0 * hop, back_ring, m, 1, hop)
        due(at + 6.5, extras_take, m, 0)
        due(at + 10.5, extras_take, m, 1)
        due(at + 15.5, extras_take, m, 2)
        due(at + 24.2, extras_rest, m)
        due(at + 26.0, extras_last, m)
    for n, dy in enumerate(y_order):
        due(25.1 + 1.4 * n, group_forward, gid_of(dy))
        due(30.6 + 1.4 * n, x_arrival, 0, dy)
        due(30.7 + 1.4 * n, group_forward, gid_of(dy, 1))

    def forward_e():
        activate(LANES, ea[...].reshape(LANES, D), slope_at_e, pool_at_e)

    due(36.5, forward_e)
    for act in sorted(steps):
        act[2](*act[3])
    sums = dot_nn(pmask[...], x_ref[...])
    acc[...] = jnp.zeros_like(acc)
    for dy in y_order:
        group_out(gid_of(dy))
    for dy in y_order:
        x_arrival(1, dy)
        group_out(gid_of(dy, 1))
    acc[...] += dot_nn(pair(pooled_e[...]), eb[...].reshape(LANES, D))
    sums = sums + acc[0:8, :] + acc[8:16, :]

    seg = lax.broadcasted_iota(jnp.int32, (8, D), 0)
    first = jnp.sum(sums[0:4], axis=0, keepdims=True)
    second = jnp.sum(sums[4:8], axis=0, keepdims=True)
    sums = jnp.where(is_text, sums, jnp.where(seg < 4, first, second))
    value = sums / count
    norm = jnp.sqrt(jnp.sum(value * value, axis=-1, keepdims=True) + norm_eps)
    unit = value / norm

    key_at = lax.broadcasted_iota(jnp.int32, (8, LANES), 0)
    key_lane = lax.broadcasted_iota(jnp.int32, (8, LANES), 1)
    group = jnp.minimum(tower, 2)
    image_key = jnp.where(key_at == 0, positive_ref[2 * group], positive_ref[2 * group + 1])
    key = jnp.where(is_text, 8 * blk + key_at, image_key)
    key = jnp.where(key_lane == 0, key >> 4, jnp.where(key_lane == 1, key & 15, 0)).astype(f32)
    keyed = jnp.concatenate([unit, key], axis=1)
    half = KEYED // 2
    tile_t[...] = jnp.concatenate([keyed[:, :half], keyed[:, half:]], axis=0).astype(bf16)
    two = jnp.concatenate([jnp.concatenate([unit[0:1], unit[4:5]], axis=0), key[0:2]], axis=1)
    fifth = KEYED // 5
    parts = [two[:, p * fifth : (p + 1) * fifth] for p in range(5)]
    tile_i[...] = jnp.concatenate(parts + [jnp.zeros((6, fifth), f32)], axis=0).astype(bf16)

    def to_column(text, d):
        if text:
            src, dst = tile_t, column_t.at[x_lo]
        else:
            src, dst = tile_i, column_i.at[x_lo * 3 + tower]
        return pltpu.make_async_remote_copy(
            src_ref=src, dst_ref=dst, send_sem=c_send.at[d - 1], recv_sem=c_recv.at[role],
            device_id=in_column(d), device_id_type=MESH,
        )

    @pl.when(is_text)
    def _():
        for d in range(1, 8):
            to_column(True, d).start()
        column_t[x_lo] = tile_t[...]

    @pl.when(jnp.logical_not(is_text))
    def _():
        for d in range(1, 8):
            to_column(False, d).start()
        column_i[x_lo * 3 + tower] = tile_i[...]

    def place_of(q):
        qx, qc = q // 2, q % 2
        g = (qx // 2) * 2 + qc
        return g == 3, qx % 2 if g == 3 else (qx % 2) * 3 + g

    for q in range(8):
        text, place = place_of(q)

        @pl.when(role != q)
        def _():
            arrived(column_t if text else column_i, place, c_recv.at[q])

    rows = []
    for k in range(2):
        v = column_t[k].astype(f32)
        rows.append(jnp.concatenate([v[0:8], v[8:16]], axis=1))
    bundle[0:16, :] = jnp.concatenate(rows, axis=0).astype(bf16)
    rows = []
    for k in range(6):
        v = column_i[k].astype(f32)
        rows.append(jnp.concatenate([v[2 * p : 2 * p + 2] for p in range(5)], axis=1))
    rows.append(jnp.zeros((4, KEYED), f32))
    bundle[16:32, :] = jnp.concatenate(rows, axis=0).astype(bf16)

    for d in range(1, N_Y):
        copy = pltpu.make_async_remote_copy(
            src_ref=bundle, dst_ref=others.at[d], send_sem=o_send.at[d], recv_sem=o_recv.at[d],
            device_id=far_to(d), device_id_type=MESH,
        )
        copy.start()
        pending.append(copy)

    def straight():
        return pltpu.make_async_remote_copy(
            src_ref=bundle, dst_ref=others.at[0], send_sem=o_send.at[0], recv_sem=o_recv.at[0],
            device_id=far_to(0), device_id_type=MESH,
        )

    @pl.when(role != 0)
    def _():
        copy = straight()
        copy.start()
        copy.wait()

    @pl.when(role == 0)
    def _():
        others[0] = bundle[...]

    for d in range(1, N_Y):
        arrived(others, d, o_recv.at[d])

    scale = scale_ref[0]
    bias = bias_ref[0]
    far = others[...].reshape(N_Y * 32, KEYED)
    logits = scale * dot_nt(bundle[:, :D], far[:, :D]) + bias
    lane = lax.broadcasted_iota(jnp.int32, (32, LANES), 1)
    place = lax.broadcasted_iota(jnp.int32, (32, LANES), 0)
    base = jnp.where(lane == 0, 16.0, jnp.where(lane == 1, 1.0, 0.0)).astype(bf16)
    key_col = dot_nt(base, far[:, D:])
    key_row = dot_nt(bundle[:, D:], jnp.concatenate([base] * 4, axis=0))
    lane32 = lax.rem(lane, 32)
    row_text, col_text = place < 16, lane32 < 16
    row_image = jnp.logical_and(place >= 16, place < 28)
    col_image = jnp.logical_and(lane32 >= 16, lane32 < 28)
    cross = jnp.logical_or(
        jnp.logical_and(row_text, col_image), jnp.logical_and(row_image, col_text)
    )
    match = jnp.where(key_col == key_row, 1.0, 0.0)
    coef = jnp.where(cross, loss_scale * (jax.nn.sigmoid(logits) - match), 0.0).astype(bf16)
    share = scale * dot_nn(coef, far[:, :D])
    third = D // 3
    for k in range(2):
        part_t[k] = share[8 * k : 8 * k + 8]
    for k in range(6):
        v = share[16 + 2 * k : 18 + 2 * k]
        v = [v[:, p * third : (p + 1) * third] for p in range(3)] + [jnp.zeros((2, third), f32)]
        part_i[k] = jnp.concatenate(v, axis=0)

    def to_owner(q):
        text, place = place_of(q)
        src, dst = (part_t, gsum_t) if text else (part_i, gsum_i)
        return pltpu.make_async_remote_copy(
            src_ref=src.at[place], dst_ref=dst.at[role], send_sem=g_send.at[q], recv_sem=g_recv.at[role],
            device_id=device_of(q // 2, y, z, q % 2), device_id_type=MESH,
        )

    for q in range(8):

        @pl.when(role != q)
        def _():
            to_owner(q).start()

    @pl.when(is_text)
    def _():
        gsum_t[role] = part_t[x_lo]
        for d in range(1, 8):
            q = lax.rem(role + d, 8)
            arrived(gsum_t, q, g_recv.at[q])
        v = gsum_t[0]
        for q in range(1, 8):
            v = v + gsum_t[q]
        grad_at[...] = v

    @pl.when(jnp.logical_not(is_text))
    def _():
        gsum_i[role] = part_i[x_lo * 3 + tower]
        for d in range(1, 8):
            q = lax.rem(role + d, 8)
            arrived(gsum_i, q, g_recv.at[q])
        v = gsum_i[0]
        for q in range(1, 8):
            v = v + gsum_i[q]
        v = jnp.concatenate([v[2 * p : 2 * p + 2] for p in range(3)], axis=1)
        grad_at[...] = jnp.where(seg < 4, v[0:1], v[1:2])

    grad = grad_at[...]
    grad = (grad - unit * jnp.sum(unit * grad, axis=-1, keepdims=True)) / norm
    grad = grad / count
    grad_rows = grad.astype(bf16)

    def back(width, weights, slope_of, at):
        gh = dot_nt(grad_rows, weights)
        for j in range(8):
            rows = slice(j * SEG, (j + 1) * SEG)
            gpre[rows, at : at + width] = (slope_of(rows) * gh[j : j + 1, :]).astype(bf16)

    for g in range(8):
        back(GROUP, wb[g].reshape(GROUP, D), lambda rows, g=g: slope[g, rows, :], g * GROUP)
    back(LANES, eb[...].reshape(LANES, D), lambda rows: slope_e[rows, :], 8 * GROUP)
    out_ref[...] = dot_nn(gpre[:, : 8 * GROUP], wa[...].reshape(8 * GROUP, D)) + dot_nn(
        gpre[:, 8 * GROUP :], ea[...].reshape(LANES, D)
    )
    for j in range(8):
        rows = slice(j * SEG, (j + 1) * SEG)
        standard, inv_std = normalise(x_ref[rows, :])
        grad_std = out_ref[rows, :] * gain
        m1 = jnp.mean(grad_std, axis=-1, keepdims=True)
        m2 = jnp.mean(grad_std * standard, axis=-1, keepdims=True)
        out_ref[rows, :] = grad[j : j + 1, :] * mask_of(rows, D) + inv_std * (
            grad_std - m1 - standard * m2
        )
    for copy in pending:
        copy.wait_send()

    @pl.when(is_text)
    def _():
        for d in range(1, 8):
            to_column(True, d).wait_send()

    @pl.when(jnp.logical_not(is_text))
    def _():
        for d in range(1, 8):
            to_column(False, d).wait_send()

    for q in range(8):

        @pl.when(role != q)
        def _():
            to_owner(q).wait_send()


def body(layer_input, caption_ids, positives, ln_gain, w_first, w_second, logit_scale, logit_bias):
    vmem = pl.BlockSpec(memory_space=pltpu.VMEM)
    smem = pl.BlockSpec(memory_space=pltpu.SMEM)
    dma = pltpu.SemaphoreType.DMA
    return pl.pallas_call(
        kernel,
        out_shape=jax.ShapeDtypeStruct((ROWS, D), f32),
        in_specs=[vmem] * 5 + [smem] * 3,
        out_specs=vmem,
        scratch_shapes=[
            pltpu.VMEM((8, N_Z, MAIN, D), bf16),
            pltpu.VMEM((8, N_Z, MAIN, D), bf16),
            pltpu.VMEM((8, EXTRA, D), bf16),
            pltpu.VMEM((8, EXTRA, D), bf16),
            pltpu.VMEM((6, EXTRA, D), bf16),
            pltpu.VMEM((6, EXTRA, D), bf16),
            pltpu.VMEM((ROWS, D), bf16),
            pltpu.VMEM((ROWS, GROUP), f32),
            pltpu.VMEM((8, ROWS, GROUP), f32),
            pltpu.VMEM((ROWS, LANES), f32),
            pltpu.VMEM((8, 8, GROUP), f32),
            pltpu.VMEM((8, LANES), f32),
            pltpu.VMEM((16, D), f32),
            pltpu.VMEM((8, ROWS), bf16),
            pltpu.VMEM((ROWS, LANES), f32),
            pltpu.VMEM((16, KEYED // 2), bf16),
            pltpu.VMEM((16, KEYED // 5), bf16),
            pltpu.VMEM((2, 16, KEYED // 2), bf16),
            pltpu.VMEM((6, 16, KEYED // 5), bf16),
            pltpu.VMEM((32, KEYED), bf16),
            pltpu.VMEM((N_Y, 32, KEYED), bf16),
            pltpu.VMEM((2, 8, D), f32),
            pltpu.VMEM((6, 8, D // 3), f32),
            pltpu.VMEM((8, 8, D), f32),
            pltpu.VMEM((8, 8, D // 3), f32),
            pltpu.VMEM((8, D), f32),
            pltpu.VMEM((ROWS, 8 * GROUP + LANES), bf16),
            dma((2, 8, 8)),
            dma((2, 4)),
            dma((2,)),
            dma((2, 2, 8)),
            dma((2, 3)),
            dma((2,)),
            dma((2, 2, 4)),
            dma((2, 2, 3)),
            dma((2, 3)),
            dma((2, 8)),
            dma((2, 7)),
            dma((2, 3)),
            dma((2, 3, 8)),
            dma((2, 3)),
            dma((2, 4, 8)),
            dma((2, 4)),
            dma((7,)),
            dma((8,)),
            dma((4,)),
            dma((4,)),
            dma((8,)),
            dma((8,)),
        ],
        compiler_params=pltpu.CompilerParams(
            collective_id=0, has_side_effects=True, vmem_limit_bytes=56 * 2**20
        ),
        name="step",
    )(
        layer_input, caption_ids, ln_gain, jnp.transpose(w_first, (2, 0, 1)), jnp.transpose(w_second, (1, 0, 2)),
        positives, logit_scale, logit_bias,
    )


def solution(mesh):
    placed = (
        P(("blk", "tower"), None),
        P("blk", None),
        P("blk"),
        P(),
        P(None, None, "blk"),
        P(None, "blk", None),
        P(),
        P(),
    )
    return jax.shard_map(
        body, mesh=mesh, in_specs=placed, out_specs=P(("blk", "tower"), None), check_vma=False
    )
```

```python
import functools

import jax
import jax.numpy as jnp
from jax import lax
from jax.experimental import pallas as pl
from jax.experimental.pallas import tpu as pltpu
from jax.sharding import PartitionSpec as P

D = 1152
ROWS = 512
N_Y = 4
N_Z = 8
MAIN = 32
GROUP = N_Z * MAIN
EXTRA = 16
SEG = 64
LANES = 128
KEYED = D + LANES
FRONT = 768
SECOND = 22.0

norm_eps = 1e-06
loss_scale = 128.0
gelu_c = 0.7978845608028654
gelu_k = gelu_c * 0.044715

MESH = pl.DeviceIdType.MESH
bf16 = jnp.bfloat16
f32 = jnp.float32


def dot_nt(left, right):
    return lax.dot_general(left, right, (((1,), (1,)), ((), ())), preferred_element_type=f32)


def dot_nn(left, right):
    return jnp.dot(left, right, preferred_element_type=f32)


def device_of(x, y, z, core):
    x = lax.rem(x + 8, 4)
    y = lax.rem(y + 8, N_Y)
    z = lax.rem(z + 16, N_Z)
    return (lax.rem(x, 2) * (N_Y * N_Z) + y * N_Z + z, (x // 2) * 2 + core)


def normalise(rows):
    values = rows.astype(f32)
    centered = values - jnp.mean(values, axis=-1, keepdims=True)
    variance = jnp.mean(centered * centered, axis=-1, keepdims=True)
    inv_std = lax.rsqrt(variance + norm_eps)
    return centered * inv_std, inv_std


def kernel(
    x_hbm, ids_hbm, gain_hbm, w1_hbm, w2_hbm, positive_ref, scale_ref, bias_ref,
    out_hbm,
    x_ref, ids_ref, gain_ref, w1_ref, w2_ref, out_ref, in_sem, out_sem,
    wa, wb, ea, eb, exa, exb, normed, pre, slope, slope_e, pooled, pooled_e, acc,
    pmask, rowmask, tile_t, tile_i, column_t, column_i, bundle, others,
    part_t, part_i, gsum_t, gsum_i, grad_at, gpre,
    recv_main, recv_by, recv_bx, recv_bz, send_by, send_bx, send_bl, send_bs, recv_ex, recv_e, send_zm, send_ze, send_ym, send_ye, send_xm, send_xe,
    c_send, c_recv, o_send, o_recv, g_send, g_recv,
):
    blk = lax.axis_index("blk")
    tower = lax.axis_index("tower")
    x_lo = blk // (N_Y * N_Z)
    y = lax.rem(blk // N_Z, N_Y)
    z = lax.rem(blk, N_Z)
    x_hi = tower // 2
    core = lax.rem(tower, 2)
    x = x_hi * 2 + x_lo
    is_text = tower == 3
    t = jnp.where(is_text, 1, 0)
    role = x * 2 + core
    gid = x_lo * N_Y + y

    def far_at(k):
        side = 1 - 2 * core
        odd = lax.rem(x, 2)
        dy = jnp.where(odd == 1, 2 * (k // 2) + x // 2, k)
        dz = jnp.where(odd == 1, side * (1 + 2 * (k % 2)), jnp.where(x == 0, 4 * core, 2 * side))
        return dy, dz

    def far_from(k):
        dy, dz = far_at(k)
        return device_of(x, y - dy, z + dz, core)

    def far_to(k):
        dy, dz = far_at(k)
        return device_of(x, y + dy, z - dz, core)

    toward = jnp.where(core == 1, 1 - 2 * x_lo, 2 * x_lo - 1)
    partner = device_of(x + toward, y, z, core)

    def ring_z(d):
        return device_of(x, y, z + d, core)

    def ring_y(d):
        return device_of(x, y + d, z, core)

    def in_column(d):
        q = lax.rem(role + d, 8)
        return device_of(q // 2, y, z, lax.rem(q, 2))

    loads = [
        pltpu.make_async_copy(src, dst, in_sem.at[k])
        for k, (src, dst) in enumerate(
            ((w1_hbm, w1_ref), (w2_hbm, w2_ref), (ids_hbm, ids_ref), (gain_hbm, gain_ref), (x_hbm, x_ref))
        )
    ]
    for load in loads:
        load.start()

    barrier = pltpu.get_barrier_semaphore()
    for d in range(1, N_Z):
        pl.semaphore_signal(barrier, inc=1, device_id=ring_z(d), device_id_type=MESH)
    for d in range(1, N_Y):
        pl.semaphore_signal(barrier, inc=1, device_id=ring_y(d), device_id_type=MESH)
    for d in range(1, 8):
        pl.semaphore_signal(barrier, inc=1, device_id=in_column(d), device_id_type=MESH)
    for k in range(1, N_Y):
        pl.semaphore_signal(barrier, inc=1, device_id=far_from(k), device_id_type=MESH)

    @pl.when(role != 0)
    def _():
        pl.semaphore_signal(barrier, inc=1, device_id=far_from(0), device_id_type=MESH)

    row = lax.broadcasted_iota(jnp.int32, (MAIN + EXTRA, 68), 0)
    col = lax.broadcasted_iota(jnp.int32, (MAIN + EXTRA, 68), 1)
    lead = jnp.logical_and(row < MAIN, 2 * row + t == col)
    rest = jnp.logical_and(col >= 2 * MAIN, 2 * (row - 2 * z) + t == col)
    pick = jnp.where(jnp.logical_or(lead, rest), 1.0, 0.0).astype(bf16)
    for load, ref, w, ex in ((loads[0], w1_ref, wa, exa), (loads[1], w2_ref, wb, exb)):
        load.wait()
        own = dot_nn(pick, ref[...].reshape(68, D)).astype(bf16)
        w[gid, z] = own[:MAIN]
        ex[0] = own[MAIN:]

    pl.semaphore_wait(barrier, jnp.where(role == 0, 20, 21))

    pending = []

    def send(ref, at, send_sem, recv_sem, target):
        copy = pltpu.make_async_remote_copy(
            src_ref=ref.at[at], dst_ref=ref.at[at], send_sem=send_sem, recv_sem=recv_sem,
            device_id=target, device_id_type=MESH,
        )
        copy.start()
        pending.append(copy)

    def arrived(ref, at, recv_sem):
        pltpu.make_async_remote_copy(
            src_ref=ref.at[at], dst_ref=ref.at[at], send_sem=recv_sem, recv_sem=recv_sem,
            device_id=partner, device_id_type=MESH,
        ).wait_recv()

    mats = ((wa, ea, exa), (wb, eb, exb))
    z_order = (0, 1, 7, 2, 6, 3, 5, 4)
    y_order = (0, 1, 3, 2)

    def zid(d):
        return lax.rem(z + d, N_Z)

    def gid_of(dy, other=0):
        half = 1 - x_lo if other else x_lo
        return half * N_Y + lax.rem(y + dy, N_Y)

    front = pl.ds(0, FRONT)
    back_cols = pl.ds(FRONT, D - FRONT)
    every = pl.ds(0, MAIN)
    long = 1 - 2 * core

    def half_of(other):
        return pl.ds((1 - x_lo if other else x_lo) * N_Y, N_Y)

    def send_z(m):
        for d in z_order[1:]:
            send(mats[m][0], (gid, z, every, front), send_zm.at[m, d - 1], recv_main.at[m, gid, z], ring_z(d))

    def send_x(m, dy, d):
        g, zz = gid_of(dy), zid(d)
        send(mats[m][0], (g, zz, every, front), send_xm.at[m, dy, d], recv_main.at[m, g, zz], partner)

    def send_y(m, d):
        zz = zid(d)
        for dy in (1, 3, 2):
            send(
                mats[m][0], (gid, zz, every, front), send_ym.at[m, dy - 1, d], recv_main.at[m, gid, zz], ring_y(dy)
            )

    def take(m, dy, other, d):
        g, zz = gid_of(dy, other), zid(d)
        arrived(mats[m][0], (g, zz, every, front), recv_main.at[m, g, zz])

    def back_y(m):
        for dy in (1, 3, 2):
            send(mats[m][0], (gid, z, every, back_cols), send_by.at[m, dy - 1], recv_by.at[m, y], ring_y(dy))

    def back_ring(m, other, hop):
        at = lambda zz: (half_of(other), zz, every, back_cols)
        h = 1 if other else 0
        w = mats[m][0]
        there = lax.rem(z - long * hop + 2 * N_Z, N_Z)
        here = lax.rem(z + long * hop + 2 * N_Z, N_Z)
        half = 1 - x_lo if other else x_lo
        if 0 < hop:
            arrived(w, at(there), recv_bz.at[m, half, there])
            if hop < 4:
                arrived(w, at(here), recv_bz.at[m, half, here])
        if hop < 4:
            send(w, at(there), send_bl.at[m, h, hop], recv_bz.at[m, half, there], ring_z(long))
        if hop < 3:
            send(w, at(here), send_bs.at[m, h, hop], recv_bz.at[m, half, here], ring_z(-long))

    def back_own(m):
        w = mats[m][0]
        for dy in (1, 3, 2):
            yy = lax.rem(y + dy, N_Y)
            arrived(w, (gid_of(dy), z, every, back_cols), recv_by.at[m, yy])
        send(w, (half_of(0), z, every, back_cols), send_bx.at[m], recv_bx.at[m], partner)
        back_ring(m, 0, 0)

    def back_partner(m):
        arrived(mats[m][0], (half_of(1), z, every, back_cols), recv_bx.at[m])
        back_ring(m, 1, 0)

    def extras_send(m, k):
        w, e, ex = mats[m]
        bit = 1 << k
        other = z + bit - 2 * bit * lax.rem(z // bit, 2)
        copy = pltpu.make_async_remote_copy(
            src_ref=ex.at[2 * k], dst_ref=ex.at[2 * k + 1], send_sem=send_ze.at[m, k],
            recv_sem=recv_ex.at[m, k], device_id=device_of(x, y, other, core), device_id_type=MESH,
        )
        copy.start()
        pending.append(copy)

    def extras_take(m, k):
        w, e, ex = mats[m]
        arrived(ex, 2 * k + 1, recv_ex.at[m, k])
        total = (ex[2 * k].astype(f32) + ex[2 * k + 1].astype(f32)).astype(bf16)
        if k < 2:
            ex[2 * k + 2] = total
            extras_send(m, k + 1)
            return
        e[gid] = total
        for dy in (1, 3, 2):
            send(e, gid, send_ye.at[m, dy - 1], recv_e.at[m, gid], ring_y(dy))
        send(e, gid, send_xe.at[m, 0], recv_e.at[m, gid], partner)

    def extras_x(m, dy):
        w, e, ex = mats[m]
        g = gid_of(dy)
        arrived(e, g, recv_e.at[m, g])
        send(e, g, send_xe.at[m, dy], recv_e.at[m, g], partner)


    def activate(width, weights, slope_at, pool_at):
        pre[:, :width] = dot_nt(normed[...], weights)

        def step(k, carry):
            rows = pl.ds(k * SEG, SEG)
            p = pre[rows, :width]
            u = p * p
            h = 0.5 + 0.5 * jnp.tanh(p * (gelu_c + gelu_k * u))
            value = p * h
            hidden[rows, :width] = value.astype(bf16)
            s = h + value * ((1.0 - h) * (2.0 * gelu_c + 6.0 * gelu_k * u))
            slope_at(rows, s * mask_of(rows, width))
            return carry

        lax.fori_loop(0, ROWS // SEG, step, 0)
        pool_at(dot_nn(pmask[...], hidden[:, :width]))

    hidden = gpre

    def group_forward(g):
        def slope_at(rows, s):
            slope[g, rows, :] = s

        def pool_at(v):
            pooled[g] = v

        activate(GROUP, wa[g].reshape(GROUP, D), slope_at, pool_at)

    def pair(v):
        hi = v.astype(bf16)
        lo = (v - hi.astype(f32)).astype(bf16)
        return jnp.concatenate([hi, lo], axis=0)

    def group_out(g):
        acc[...] += dot_nn(pair(pooled[g]), wb[g].reshape(GROUP, D))

    def slope_at_e(rows, s):
        slope_e[rows, :] = s

    def pool_at_e(v):
        pooled_e[...] = v

    def norm_block(j):
        standard, _ = normalise(x_ref[pl.ds(j * SEG, SEG), :])
        normed[pl.ds(j * SEG, SEG), :] = (standard * gain).astype(bf16)

    steps = []

    def due(when, act, *args):
        steps.append((when, len(steps), act, args))

    def start(m):
        send_z(m)
        back_y(m)
        send_y(m, 0)
        send_x(m, 0, 0)
        extras_send(m, 0)

    def z_arrival(m, d):
        take(m, 0, 0, d)
        send_y(m, d)
        send_x(m, 0, d)

    def y_arrival(m, d):
        for dy in y_order[1:]:
            take(m, dy, 0, d)
            send_x(m, dy, d)

    def x_arrival(m, dy):
        for d in z_order:
            take(m, dy, 1, d)

    def extras_rest(m):
        for dy in y_order[1:]:
            extras_x(m, dy)

    def extras_last(m):
        for dy in y_order:
            arrived(mats[m][1], gid_of(dy, 1), recv_e.at[m, gid_of(dy, 1)])

    start(0)
    for load in loads[2:]:
        load.wait()
    gain = gain_ref[pl.ds(t, 1), :]

    mask = jnp.where(is_text, jnp.where(ids_ref[...] != 0, 1.0, 0.0), 1.0)
    count = jnp.where(is_text, jnp.sum(mask, axis=1, keepdims=True), 256.0)
    slot = lax.broadcasted_iota(jnp.int32, (SEG, ROWS), 0)
    at = lax.broadcasted_iota(jnp.int32, (SEG, ROWS), 1)
    spread = jnp.where(lax.rem(at, SEG) == slot, 1.0, 0.0).astype(bf16)
    wide = dot_nn(mask.astype(bf16), spread)
    segment = lax.broadcasted_iota(jnp.int32, (8, ROWS), 0)
    at = lax.broadcasted_iota(jnp.int32, (8, ROWS), 1)
    pmask[...] = jnp.where(at // SEG == segment, wide, 0.0).astype(bf16)
    rowmask[...] = lax.dot_general(
        pmask[...], jnp.ones((8, LANES), bf16), (((0,), (0,)), ((), ())), preferred_element_type=f32
    )

    def mask_of(rows, width):
        return jnp.concatenate([rowmask[rows, :]] * (width // LANES), axis=1)

    for j in range(8):
        due(13.0 + 1.2 * j, norm_block, j)
    for m, at in ((0, 0.0), (1, SECOND)):
        if m:
            due(at, start, m)
        for n, d in enumerate(z_order[1:]):
            due(at + 4.4 + 1.3 * n, z_arrival, m, d)
        for n, d in enumerate(z_order):
            due(at + 7.0 + 2.3 * n, y_arrival, m, d)
        due(at + 5.0, back_own, m)
        due(at + 8.0, back_partner, m)
        for hop in range(1, 5):
            due(at + 6.0 + 5.0 * hop, back_ring, m, 0, hop)
            due(at + 9.0 + 5.0 * hop, back_ring, m, 1, hop)
        due(at + 6.5, extras_take, m, 0)
        due(at + 10.5, extras_take, m, 1)
        due(at + 15.5, extras_take, m, 2)
        due(at + 24.2, extras_rest, m)
        due(at + 26.0, extras_last, m)
    for n, dy in enumerate(y_order):
        due(26.1 + 1.4 * n, group_forward, gid_of(dy))
        due(31.6 + 1.4 * n, x_arrival, 0, dy)
        due(31.7 + 1.4 * n, group_forward, gid_of(dy, 1))

    def forward_e():
        activate(LANES, ea[...].reshape(LANES, D), slope_at_e, pool_at_e)

    due(37.5, forward_e)
    for act in sorted(steps):
        act[2](*act[3])
    sums = dot_nn(pmask[...], x_ref[...])
    acc[...] = jnp.zeros_like(acc)
    for dy in y_order:
        group_out(gid_of(dy))
    for dy in y_order:
        x_arrival(1, dy)
        group_out(gid_of(dy, 1))
    acc[...] += dot_nn(pair(pooled_e[...]), eb[...].reshape(LANES, D))
    sums = sums + acc[0:8, :] + acc[8:16, :]

    seg = lax.broadcasted_iota(jnp.int32, (8, D), 0)
    first = jnp.sum(sums[0:4], axis=0, keepdims=True)
    second = jnp.sum(sums[4:8], axis=0, keepdims=True)
    sums = jnp.where(is_text, sums, jnp.where(seg < 4, first, second))
    value = sums / count
    norm = jnp.sqrt(jnp.sum(value * value, axis=-1, keepdims=True) + norm_eps)
    unit = value / norm

    key_at = lax.broadcasted_iota(jnp.int32, (8, LANES), 0)
    key_lane = lax.broadcasted_iota(jnp.int32, (8, LANES), 1)
    group = jnp.minimum(tower, 2)
    image_key = jnp.where(key_at == 0, positive_ref[2 * group], positive_ref[2 * group + 1])
    key = jnp.where(is_text, 8 * blk + key_at, image_key)
    key = jnp.where(key_lane == 0, key >> 4, jnp.where(key_lane == 1, key & 15, 0)).astype(f32)
    keyed = jnp.concatenate([unit, key], axis=1)
    half = KEYED // 2
    tile_t[...] = jnp.concatenate([keyed[:, :half], keyed[:, half:]], axis=0).astype(bf16)
    two = jnp.concatenate([jnp.concatenate([unit[0:1], unit[4:5]], axis=0), key[0:2]], axis=1)
    fifth = KEYED // 5
    parts = [two[:, p * fifth : (p + 1) * fifth] for p in range(5)]
    tile_i[...] = jnp.concatenate(parts + [jnp.zeros((6, fifth), f32)], axis=0).astype(bf16)

    def to_column(text, d):
        if text:
            src, dst = tile_t, column_t.at[x_lo]
        else:
            src, dst = tile_i, column_i.at[x_lo * 3 + tower]
        return pltpu.make_async_remote_copy(
            src_ref=src, dst_ref=dst, send_sem=c_send.at[d - 1], recv_sem=c_recv.at[role],
            device_id=in_column(d), device_id_type=MESH,
        )

    @pl.when(is_text)
    def _():
        for d in range(1, 8):
            to_column(True, d).start()
        column_t[x_lo] = tile_t[...]

    @pl.when(jnp.logical_not(is_text))
    def _():
        for d in range(1, 8):
            to_column(False, d).start()
        column_i[x_lo * 3 + tower] = tile_i[...]

    def place_of(q):
        qx, qc = q // 2, q % 2
        g = (qx // 2) * 2 + qc
        return g == 3, qx % 2 if g == 3 else (qx % 2) * 3 + g

    for q in range(8):
        text, place = place_of(q)

        @pl.when(role != q)
        def _():
            arrived(column_t if text else column_i, place, c_recv.at[q])

    rows = []
    for k in range(2):
        v = column_t[k].astype(f32)
        rows.append(jnp.concatenate([v[0:8], v[8:16]], axis=1))
    bundle[0:16, :] = jnp.concatenate(rows, axis=0).astype(bf16)
    rows = []
    for k in range(6):
        v = column_i[k].astype(f32)
        rows.append(jnp.concatenate([v[2 * p : 2 * p + 2] for p in range(5)], axis=1))
    rows.append(jnp.zeros((4, KEYED), f32))
    bundle[16:32, :] = jnp.concatenate(rows, axis=0).astype(bf16)

    for d in range(1, N_Y):
        copy = pltpu.make_async_remote_copy(
            src_ref=bundle, dst_ref=others.at[d], send_sem=o_send.at[d], recv_sem=o_recv.at[d],
            device_id=far_to(d), device_id_type=MESH,
        )
        copy.start()
        pending.append(copy)

    def straight():
        return pltpu.make_async_remote_copy(
            src_ref=bundle, dst_ref=others.at[0], send_sem=o_send.at[0], recv_sem=o_recv.at[0],
            device_id=far_to(0), device_id_type=MESH,
        )

    @pl.when(role != 0)
    def _():
        copy = straight()
        copy.start()
        copy.wait()

    @pl.when(role == 0)
    def _():
        others[0] = bundle[...]

    for d in range(1, N_Y):
        arrived(others, d, o_recv.at[d])

    scale = scale_ref[0]
    bias = bias_ref[0]
    far = others[...].reshape(N_Y * 32, KEYED)
    logits = scale * dot_nt(bundle[:, :D], far[:, :D]) + bias
    lane = lax.broadcasted_iota(jnp.int32, (32, LANES), 1)
    place = lax.broadcasted_iota(jnp.int32, (32, LANES), 0)
    base = jnp.where(lane == 0, 16.0, jnp.where(lane == 1, 1.0, 0.0)).astype(bf16)
    key_col = dot_nt(base, far[:, D:])
    key_row = dot_nt(bundle[:, D:], jnp.concatenate([base] * 4, axis=0))
    lane32 = lax.rem(lane, 32)
    row_text, col_text = place < 16, lane32 < 16
    row_image = jnp.logical_and(place >= 16, place < 28)
    col_image = jnp.logical_and(lane32 >= 16, lane32 < 28)
    cross = jnp.logical_or(
        jnp.logical_and(row_text, col_image), jnp.logical_and(row_image, col_text)
    )
    match = jnp.where(key_col == key_row, 1.0, 0.0)
    coef = jnp.where(cross, loss_scale * (jax.nn.sigmoid(logits) - match), 0.0).astype(bf16)
    share = scale * dot_nn(coef, far[:, :D])
    third = D // 3
    for k in range(2):
        part_t[k] = share[8 * k : 8 * k + 8]
    for k in range(6):
        v = share[16 + 2 * k : 18 + 2 * k]
        v = [v[:, p * third : (p + 1) * third] for p in range(3)] + [jnp.zeros((2, third), f32)]
        part_i[k] = jnp.concatenate(v, axis=0)

    def to_owner(q):
        text, place = place_of(q)
        src, dst = (part_t, gsum_t) if text else (part_i, gsum_i)
        return pltpu.make_async_remote_copy(
            src_ref=src.at[place], dst_ref=dst.at[role], send_sem=g_send.at[q], recv_sem=g_recv.at[role],
            device_id=device_of(q // 2, y, z, q % 2), device_id_type=MESH,
        )

    for q in range(8):

        @pl.when(role != q)
        def _():
            to_owner(q).start()

    @pl.when(is_text)
    def _():
        gsum_t[role] = part_t[x_lo]
        for d in range(1, 8):
            q = lax.rem(role + d, 8)
            arrived(gsum_t, q, g_recv.at[q])
        v = gsum_t[0]
        for q in range(1, 8):
            v = v + gsum_t[q]
        grad_at[...] = v

    @pl.when(jnp.logical_not(is_text))
    def _():
        gsum_i[role] = part_i[x_lo * 3 + tower]
        for d in range(1, 8):
            q = lax.rem(role + d, 8)
            arrived(gsum_i, q, g_recv.at[q])
        v = gsum_i[0]
        for q in range(1, 8):
            v = v + gsum_i[q]
        v = jnp.concatenate([v[2 * p : 2 * p + 2] for p in range(3)], axis=1)
        grad_at[...] = jnp.where(seg < 4, v[0:1], v[1:2])

    grad = grad_at[...]
    grad = (grad - unit * jnp.sum(unit * grad, axis=-1, keepdims=True)) / norm
    grad = grad / count
    grad_rows = grad.astype(bf16)

    def back(width, weights, slope_of, at):
        gh = dot_nt(grad_rows, weights)
        for j in range(8):
            rows = slice(j * SEG, (j + 1) * SEG)
            gpre[rows, at : at + width] = (slope_of(rows) * gh[j : j + 1, :]).astype(bf16)

    for g in range(8):
        back(GROUP, wb[g].reshape(GROUP, D), lambda rows, g=g: slope[g, rows, :], g * GROUP)
    back(LANES, eb[...].reshape(LANES, D), lambda rows: slope_e[rows, :], 8 * GROUP)
    out_ref[...] = dot_nn(gpre[:, : 8 * GROUP], wa[...].reshape(8 * GROUP, D)) + dot_nn(
        gpre[:, 8 * GROUP :], ea[...].reshape(LANES, D)
    )
    for j in range(8):
        rows = slice(j * SEG, (j + 1) * SEG)
        standard, inv_std = normalise(x_ref[rows, :])
        grad_std = out_ref[rows, :] * gain
        m1 = jnp.mean(grad_std, axis=-1, keepdims=True)
        m2 = jnp.mean(grad_std * standard, axis=-1, keepdims=True)
        out_ref[rows, :] = grad[j : j + 1, :] * mask_of(rows, D) + inv_std * (
            grad_std - m1 - standard * m2
        )
        pltpu.make_async_copy(out_ref.at[rows], out_hbm.at[rows], out_sem.at[j]).start()
    for j in range(8):
        rows = slice(j * SEG, (j + 1) * SEG)
        pltpu.make_async_copy(out_ref.at[rows], out_hbm.at[rows], out_sem.at[j]).wait()
    for copy in pending:
        copy.wait_send()

    @pl.when(is_text)
    def _():
        for d in range(1, 8):
            to_column(True, d).wait_send()

    @pl.when(jnp.logical_not(is_text))
    def _():
        for d in range(1, 8):
            to_column(False, d).wait_send()

    for q in range(8):

        @pl.when(role != q)
        def _():
            to_owner(q).wait_send()


def body(layer_input, caption_ids, positives, ln_gain, w_first, w_second, logit_scale, logit_bias):
    anywhere = pl.BlockSpec(memory_space=pl.ANY)
    smem = pl.BlockSpec(memory_space=pltpu.SMEM)
    dma = pltpu.SemaphoreType.DMA
    return pl.pallas_call(
        kernel,
        out_shape=jax.ShapeDtypeStruct((ROWS, D), f32),
        in_specs=[anywhere] * 5 + [smem] * 3,
        out_specs=anywhere,
        scratch_shapes=[
            pltpu.VMEM((ROWS, D), bf16),
            pltpu.VMEM((8, SEG), jnp.int32),
            pltpu.VMEM((2, D), f32),
            pltpu.VMEM((34, 2, D), bf16),
            pltpu.VMEM((34, 2, D), bf16),
            pltpu.VMEM((ROWS, D), f32),
            dma((5,)),
            dma((8,)),
            pltpu.VMEM((8, N_Z, MAIN, D), bf16),
            pltpu.VMEM((8, N_Z, MAIN, D), bf16),
            pltpu.VMEM((8, EXTRA, D), bf16),
            pltpu.VMEM((8, EXTRA, D), bf16),
            pltpu.VMEM((6, EXTRA, D), bf16),
            pltpu.VMEM((6, EXTRA, D), bf16),
            pltpu.VMEM((ROWS, D), bf16),
            pltpu.VMEM((ROWS, GROUP), f32),
            pltpu.VMEM((8, ROWS, GROUP), f32),
            pltpu.VMEM((ROWS, LANES), f32),
            pltpu.VMEM((8, 8, GROUP), f32),
            pltpu.VMEM((8, LANES), f32),
            pltpu.VMEM((16, D), f32),
            pltpu.VMEM((8, ROWS), bf16),
            pltpu.VMEM((ROWS, LANES), f32),
            pltpu.VMEM((16, KEYED // 2), bf16),
            pltpu.VMEM((16, KEYED // 5), bf16),
            pltpu.VMEM((2, 16, KEYED // 2), bf16),
            pltpu.VMEM((6, 16, KEYED // 5), bf16),
            pltpu.VMEM((32, KEYED), bf16),
            pltpu.VMEM((N_Y, 32, KEYED), bf16),
            pltpu.VMEM((2, 8, D), f32),
            pltpu.VMEM((6, 8, D // 3), f32),
            pltpu.VMEM((8, 8, D), f32),
            pltpu.VMEM((8, 8, D // 3), f32),
            pltpu.VMEM((8, D), f32),
            pltpu.VMEM((ROWS, 8 * GROUP + LANES), bf16),
            dma((2, 8, 8)),
            dma((2, 4)),
            dma((2,)),
            dma((2, 2, 8)),
            dma((2, 3)),
            dma((2,)),
            dma((2, 2, 4)),
            dma((2, 2, 3)),
            dma((2, 3)),
            dma((2, 8)),
            dma((2, 7)),
            dma((2, 3)),
            dma((2, 3, 8)),
            dma((2, 3)),
            dma((2, 4, 8)),
            dma((2, 4)),
            dma((7,)),
            dma((8,)),
            dma((4,)),
            dma((4,)),
            dma((8,)),
            dma((8,)),
        ],
        compiler_params=pltpu.CompilerParams(
            collective_id=0, has_side_effects=True, vmem_limit_bytes=56 * 2**20
        ),
        name="step",
    )(
        layer_input, caption_ids, ln_gain, jnp.transpose(w_first, (2, 0, 1)), jnp.transpose(w_second, (1, 0, 2)),
        positives, logit_scale, logit_bias,
    )


def solution(mesh):
    placed = (
        P(("blk", "tower"), None),
        P("blk", None),
        P("blk"),
        P(),
        P(None, None, "blk"),
        P(None, "blk", None),
        P(),
        P(),
    )
    return jax.shard_map(
        body, mesh=mesh, in_specs=placed, out_specs=P(("blk", "tower"), None), check_vma=False
    )
```

```python
import functools

import jax
import jax.numpy as jnp
from jax import lax
from jax.experimental import pallas as pl
from jax.experimental.pallas import tpu as pltpu
from jax.sharding import PartitionSpec as P

D = 1152
ROWS = 512
N_Y = 4
N_Z = 8
MAIN = 32
GROUP = N_Z * MAIN
EXTRA = 16
SEG = 64
LANES = 128
KEYED = D + LANES
FRONT = 768
SECOND = 18.0

norm_eps = 1e-06
loss_scale = 128.0
gelu_c = 0.7978845608028654
gelu_k = gelu_c * 0.044715

MESH = pl.DeviceIdType.MESH
bf16 = jnp.bfloat16
f32 = jnp.float32


def dot_nt(left, right):
    return lax.dot_general(left, right, (((1,), (1,)), ((), ())), preferred_element_type=f32)


def dot_nn(left, right):
    return jnp.dot(left, right, preferred_element_type=f32)


def device_of(x, y, z, core):
    x = lax.rem(x + 8, 4)
    y = lax.rem(y + 8, N_Y)
    z = lax.rem(z + 16, N_Z)
    return (lax.rem(x, 2) * (N_Y * N_Z) + y * N_Z + z, (x // 2) * 2 + core)


def normalise(rows):
    values = rows.astype(f32)
    centered = values - jnp.mean(values, axis=-1, keepdims=True)
    variance = jnp.mean(centered * centered, axis=-1, keepdims=True)
    inv_std = lax.rsqrt(variance + norm_eps)
    return centered * inv_std, inv_std


def kernel(
    x_hbm, ids_hbm, gain_hbm, w1_hbm, w2_hbm, positive_ref, scale_ref, bias_ref,
    out_hbm,
    x_ref, ids_ref, gain_ref, w1_ref, w2_ref, out_ref, in_sem, out_sem,
    wa, wb, ea, eb, exa, exb, normed, pre, slope, slope_e, pooled, pooled_e, acc,
    pmask, rowmask, tile_t, tile_i, column_t, column_i, bundle, others,
    part_t, part_i, gsum_t, gsum_i, grad_at, gpre,
    recv_main, recv_by, recv_bx, recv_bz, send_by, send_bx, send_bl, send_bs, recv_ex, recv_e, send_zm, send_ze, send_ym, send_ye, send_xm, send_xe,
    c_send, c_recv, o_send, o_recv, g_send, g_recv,
):
    blk = lax.axis_index("blk")
    tower = lax.axis_index("tower")
    x_lo = blk // (N_Y * N_Z)
    y = lax.rem(blk // N_Z, N_Y)
    z = lax.rem(blk, N_Z)
    x_hi = tower // 2
    core = lax.rem(tower, 2)
    x = x_hi * 2 + x_lo
    is_text = tower == 3
    t = jnp.where(is_text, 1, 0)
    role = x * 2 + core
    gid = x_lo * N_Y + y

    def far_at(k):
        side = 1 - 2 * core
        odd = lax.rem(x, 2)
        dy = jnp.where(odd == 1, 2 * (k // 2) + x // 2, k)
        dz = jnp.where(odd == 1, side * (1 + 2 * (k % 2)), jnp.where(x == 0, 4 * core, 2 * side))
        return dy, dz

    def far_from(k):
        dy, dz = far_at(k)
        return device_of(x, y - dy, z + dz, core)

    def far_to(k):
        dy, dz = far_at(k)
        return device_of(x, y + dy, z - dz, core)

    toward = jnp.where(core == 1, 1 - 2 * x_lo, 2 * x_lo - 1)
    partner = device_of(x + toward, y, z, core)

    def ring_z(d):
        return device_of(x, y, z + d, core)

    def ring_y(d):
        return device_of(x, y + d, z, core)

    def in_column(d):
        q = lax.rem(role + d, 8)
        return device_of(q // 2, y, z, lax.rem(q, 2))

    loads = [
        pltpu.make_async_copy(src, dst, in_sem.at[k])
        for k, (src, dst) in enumerate(
            ((w1_hbm, w1_ref), (w2_hbm, w2_ref), (ids_hbm, ids_ref), (gain_hbm, gain_ref), (x_hbm, x_ref))
        )
    ]
    for load in loads:
        load.start()

    barrier = pltpu.get_barrier_semaphore()
    for d in range(1, N_Z):
        pl.semaphore_signal(barrier, inc=1, device_id=ring_z(d), device_id_type=MESH)
    for d in range(1, N_Y):
        pl.semaphore_signal(barrier, inc=1, device_id=ring_y(d), device_id_type=MESH)
    for d in range(1, 8):
        pl.semaphore_signal(barrier, inc=1, device_id=in_column(d), device_id_type=MESH)
    for k in range(1, N_Y):
        pl.semaphore_signal(barrier, inc=1, device_id=far_from(k), device_id_type=MESH)

    @pl.when(role != 0)
    def _():
        pl.semaphore_signal(barrier, inc=1, device_id=far_from(0), device_id_type=MESH)

    row = lax.broadcasted_iota(jnp.int32, (MAIN + EXTRA, 68), 0)
    col = lax.broadcasted_iota(jnp.int32, (MAIN + EXTRA, 68), 1)
    lead = jnp.logical_and(row < MAIN, 2 * row + t == col)
    rest = jnp.logical_and(col >= 2 * MAIN, 2 * (row - 2 * z) + t == col)
    pick = jnp.where(jnp.logical_or(lead, rest), 1.0, 0.0).astype(bf16)
    for load, ref, w, ex in ((loads[0], w1_ref, wa, exa), (loads[1], w2_ref, wb, exb)):
        load.wait()
        own = dot_nn(pick, ref[...].reshape(68, D)).astype(bf16)
        w[gid, z] = own[:MAIN]
        ex[0] = own[MAIN:]

    pl.semaphore_wait(barrier, jnp.where(role == 0, 20, 21))

    pending = []

    def send(ref, at, send_sem, recv_sem, target):
        copy = pltpu.make_async_remote_copy(
            src_ref=ref.at[at], dst_ref=ref.at[at], send_sem=send_sem, recv_sem=recv_sem,
            device_id=target, device_id_type=MESH,
        )
        copy.start()
        pending.append(copy)

    def arrived(ref, at, recv_sem):
        pltpu.make_async_remote_copy(
            src_ref=ref.at[at], dst_ref=ref.at[at], send_sem=recv_sem, recv_sem=recv_sem,
            device_id=partner, device_id_type=MESH,
        ).wait_recv()

    mats = ((wa, ea, exa), (wb, eb, exb))
    z_order = (0, 1, 7, 2, 6, 3, 5, 4)
    y_order = (0, 1, 3, 2)

    def zid(d):
        return lax.rem(z + d, N_Z)

    def gid_of(dy, other=0):
        half = 1 - x_lo if other else x_lo
        return half * N_Y + lax.rem(y + dy, N_Y)

    front = pl.ds(0, FRONT)
    back_cols = pl.ds(FRONT, D - FRONT)
    every = pl.ds(0, MAIN)
    long = 1 - 2 * core

    def half_of(other):
        return pl.ds((1 - x_lo if other else x_lo) * N_Y, N_Y)

    def send_z(m):
        for d in (1, 7, 2, 6):
            send(mats[m][0], (gid, z, every, front), send_zm.at[m, d - 1], recv_main.at[m, gid, z], ring_z(d))

    def pass_z(m, origin, slot, places):
        send(
            mats[m][0], (gid, origin, every, front), send_zm.at[m, slot], recv_main.at[m, gid, origin], ring_z(places)
        )

    def send_x(m, dy, d):
        g, zz = gid_of(dy), zid(d)
        send(mats[m][0], (g, zz, every, front), send_xm.at[m, dy, d], recv_main.at[m, g, zz], partner)

    def send_y(m, d):
        zz = zid(d)
        for dy in (1, 3, 2):
            send(
                mats[m][0], (gid, zz, every, front), send_ym.at[m, dy - 1, d], recv_main.at[m, gid, zz], ring_y(dy)
            )

    def take(m, dy, other, d):
        g, zz = gid_of(dy, other), zid(d)
        arrived(mats[m][0], (g, zz, every, front), recv_main.at[m, g, zz])

    def back_y(m):
        for dy in (1, 3, 2):
            send(mats[m][0], (gid, z, every, back_cols), send_by.at[m, dy - 1], recv_by.at[m, y], ring_y(dy))

    def back_ring(m, other, hop):
        at = lambda zz: (half_of(other), zz, every, back_cols)
        h = 1 if other else 0
        w = mats[m][0]
        there = lax.rem(z - long * hop + 2 * N_Z, N_Z)
        here = lax.rem(z + long * hop + 2 * N_Z, N_Z)
        half = 1 - x_lo if other else x_lo
        if 0 < hop:
            arrived(w, at(there), recv_bz.at[m, half, there])
            if hop < 4:
                arrived(w, at(here), recv_bz.at[m, half, here])
        if hop < 4:
            send(w, at(there), send_bl.at[m, h, hop], recv_bz.at[m, half, there], ring_z(long))
        if hop < 3:
            send(w, at(here), send_bs.at[m, h, hop], recv_bz.at[m, half, here], ring_z(-long))

    def back_own(m):
        w = mats[m][0]
        for dy in (1, 3, 2):
            yy = lax.rem(y + dy, N_Y)
            arrived(w, (gid_of(dy), z, every, back_cols), recv_by.at[m, yy])
        send(w, (half_of(0), z, every, back_cols), send_bx.at[m], recv_bx.at[m], partner)
        back_ring(m, 0, 0)

    def back_partner(m):
        arrived(mats[m][0], (half_of(1), z, every, back_cols), recv_bx.at[m])
        back_ring(m, 1, 0)

    def extras_send(m, k):
        w, e, ex = mats[m]
        bit = 1 << k
        other = z + bit - 2 * bit * lax.rem(z // bit, 2)
        copy = pltpu.make_async_remote_copy(
            src_ref=ex.at[2 * k], dst_ref=ex.at[2 * k + 1], send_sem=send_ze.at[m, k],
            recv_sem=recv_ex.at[m, k], device_id=device_of(x, y, other, core), device_id_type=MESH,
        )
        copy.start()
        pending.append(copy)

    def extras_take(m, k):
        w, e, ex = mats[m]
        arrived(ex, 2 * k + 1, recv_ex.at[m, k])
        total = (ex[2 * k].astype(f32) + ex[2 * k + 1].astype(f32)).astype(bf16)
        if k < 2:
            ex[2 * k + 2] = total
            extras_send(m, k + 1)
            return
        e[gid] = total
        for dy in (1, 3, 2):
            send(e, gid, send_ye.at[m, dy - 1], recv_e.at[m, gid], ring_y(dy))
        send(e, gid, send_xe.at[m, 0], recv_e.at[m, gid], partner)

    def extras_x(m, dy):
        w, e, ex = mats[m]
        g = gid_of(dy)
        arrived(e, g, recv_e.at[m, g])
        send(e, g, send_xe.at[m, dy], recv_e.at[m, g], partner)


    def activate(width, weights, slope_at, pool_at):
        pre[:, :width] = dot_nt(normed[...], weights)

        def step(k, carry):
            rows = pl.ds(k * SEG, SEG)
            p = pre[rows, :width]
            u = p * p
            h = 0.5 + 0.5 * jnp.tanh(p * (gelu_c + gelu_k * u))
            value = p * h
            hidden[rows, :width] = value.astype(bf16)
            s = h + value * ((1.0 - h) * (2.0 * gelu_c + 6.0 * gelu_k * u))
            slope_at(rows, s * mask_of(rows, width))
            return carry

        lax.fori_loop(0, ROWS // SEG, step, 0)
        pool_at(dot_nn(pmask[...], hidden[:, :width]))

    hidden = gpre

    def group_forward(g):
        def slope_at(rows, s):
            slope[g, rows, :] = s

        def pool_at(v):
            pooled[g] = v

        activate(GROUP, wa[g].reshape(GROUP, D), slope_at, pool_at)

    def pair(v):
        hi = v.astype(bf16)
        lo = (v - hi.astype(f32)).astype(bf16)
        return jnp.concatenate([hi, lo], axis=0)

    def group_out(g):
        acc[...] += dot_nn(pair(pooled[g]), wb[g].reshape(GROUP, D))

    def slope_at_e(rows, s):
        slope_e[rows, :] = s

    def pool_at_e(v):
        pooled_e[...] = v

    def norm_block(j):
        standard, _ = normalise(x_ref[pl.ds(j * SEG, SEG), :])
        normed[pl.ds(j * SEG, SEG), :] = (standard * gain).astype(bf16)

    steps = []

    def due(when, act, *args):
        steps.append((when, len(steps), act, args))

    def start(m):
        send_z(m)
        back_y(m)
        send_y(m, 0)
        send_x(m, 0, 0)
        extras_send(m, 0)

    def z_arrival(m, d):
        take(m, 0, 0, d)
        if d == 2:
            pass_z(m, zid(2), 2, -1)
        if d == 6:
            pass_z(m, zid(6), 4, 1)
            pass_z(m, lax.rem(z - 2 * long + 2 * N_Z, N_Z), 3, 2 * long)
        send_y(m, d)
        send_x(m, 0, d)

    def y_arrival(m, d):
        for dy in y_order[1:]:
            take(m, dy, 0, d)
            send_x(m, dy, d)

    def x_arrival(m, dy):
        for d in z_order:
            take(m, dy, 1, d)

    def extras_rest(m):
        for dy in y_order[1:]:
            extras_x(m, dy)

    def extras_last(m):
        for dy in y_order:
            arrived(mats[m][1], gid_of(dy, 1), recv_e.at[m, gid_of(dy, 1)])

    start(0)
    for load in loads[2:]:
        load.wait()
    gain = gain_ref[pl.ds(t, 1), :]

    mask = jnp.where(is_text, jnp.where(ids_ref[...] != 0, 1.0, 0.0), 1.0)
    count = jnp.where(is_text, jnp.sum(mask, axis=1, keepdims=True), 256.0)
    slot = lax.broadcasted_iota(jnp.int32, (SEG, ROWS), 0)
    at = lax.broadcasted_iota(jnp.int32, (SEG, ROWS), 1)
    spread = jnp.where(lax.rem(at, SEG) == slot, 1.0, 0.0).astype(bf16)
    wide = dot_nn(mask.astype(bf16), spread)
    segment = lax.broadcasted_iota(jnp.int32, (8, ROWS), 0)
    at = lax.broadcasted_iota(jnp.int32, (8, ROWS), 1)
    pmask[...] = jnp.where(at // SEG == segment, wide, 0.0).astype(bf16)
    rowmask[...] = lax.dot_general(
        pmask[...], jnp.ones((8, LANES), bf16), (((0,), (0,)), ((), ())), preferred_element_type=f32
    )

    def mask_of(rows, width):
        return jnp.concatenate([rowmask[rows, :]] * (width // LANES), axis=1)

    for j in range(8):
        due(13.0 + 1.2 * j, norm_block, j)
    for m, at in ((0, 0.0), (1, SECOND)):
        if m:
            due(at, start, m)
        for n, d in enumerate(z_order[1:]):
            due(at + 3.8 + 0.9 * n + (2.0 if n > 3 else 0.0), z_arrival, m, d)
        for n, d in enumerate(z_order):
            due(at + 7.0 + 2.3 * n, y_arrival, m, d)
        due(at + 5.0, back_own, m)
        due(at + 8.0, back_partner, m)
        for hop in range(1, 5):
            due(at + 6.0 + 5.0 * hop, back_ring, m, 0, hop)
            due(at + 9.0 + 5.0 * hop, back_ring, m, 1, hop)
        due(at + 6.5, extras_take, m, 0)
        due(at + 10.5, extras_take, m, 1)
        due(at + 15.5, extras_take, m, 2)
        due(at + 24.2, extras_rest, m)
        due(at + 26.0, extras_last, m)
    for n, dy in enumerate(y_order):
        due(26.1 + 1.4 * n, group_forward, gid_of(dy))
        due(31.6 + 1.4 * n, x_arrival, 0, dy)
        due(31.7 + 1.4 * n, group_forward, gid_of(dy, 1))

    def forward_e():
        activate(LANES, ea[...].reshape(LANES, D), slope_at_e, pool_at_e)

    due(37.5, forward_e)
    for act in sorted(steps):
        act[2](*act[3])
    sums = dot_nn(pmask[...], x_ref[...])
    acc[...] = jnp.zeros_like(acc)
    for dy in y_order:
        group_out(gid_of(dy))
    for dy in y_order:
        x_arrival(1, dy)
        group_out(gid_of(dy, 1))
    acc[...] += dot_nn(pair(pooled_e[...]), eb[...].reshape(LANES, D))
    sums = sums + acc[0:8, :] + acc[8:16, :]

    seg = lax.broadcasted_iota(jnp.int32, (8, D), 0)
    first = jnp.sum(sums[0:4], axis=0, keepdims=True)
    second = jnp.sum(sums[4:8], axis=0, keepdims=True)
    sums = jnp.where(is_text, sums, jnp.where(seg < 4, first, second))
    value = sums / count
    norm = jnp.sqrt(jnp.sum(value * value, axis=-1, keepdims=True) + norm_eps)
    unit = value / norm

    key_at = lax.broadcasted_iota(jnp.int32, (8, LANES), 0)
    key_lane = lax.broadcasted_iota(jnp.int32, (8, LANES), 1)
    group = jnp.minimum(tower, 2)
    image_key = jnp.where(key_at == 0, positive_ref[2 * group], positive_ref[2 * group + 1])
    key = jnp.where(is_text, 8 * blk + key_at, image_key)
    key = jnp.where(key_lane == 0, key >> 4, jnp.where(key_lane == 1, key & 15, 0)).astype(f32)
    keyed = jnp.concatenate([unit, key], axis=1)
    half = KEYED // 2
    tile_t[...] = jnp.concatenate([keyed[:, :half], keyed[:, half:]], axis=0).astype(bf16)
    two = jnp.concatenate([jnp.concatenate([unit[0:1], unit[4:5]], axis=0), key[0:2]], axis=1)
    fifth = KEYED // 5
    parts = [two[:, p * fifth : (p + 1) * fifth] for p in range(5)]
    tile_i[...] = jnp.concatenate(parts + [jnp.zeros((6, fifth), f32)], axis=0).astype(bf16)

    def to_column(text, d):
        if text:
            src, dst = tile_t, column_t.at[x_lo]
        else:
            src, dst = tile_i, column_i.at[x_lo * 3 + tower]
        return pltpu.make_async_remote_copy(
            src_ref=src, dst_ref=dst, send_sem=c_send.at[d - 1], recv_sem=c_recv.at[role],
            device_id=in_column(d), device_id_type=MESH,
        )

    @pl.when(is_text)
    def _():
        for d in range(1, 8):
            to_column(True, d).start()
        column_t[x_lo] = tile_t[...]

    @pl.when(jnp.logical_not(is_text))
    def _():
        for d in range(1, 8):
            to_column(False, d).start()
        column_i[x_lo * 3 + tower] = tile_i[...]

    def place_of(q):
        qx, qc = q // 2, q % 2
        g = (qx // 2) * 2 + qc
        return g == 3, qx % 2 if g == 3 else (qx % 2) * 3 + g

    for q in range(8):
        text, place = place_of(q)

        @pl.when(role != q)
        def _():
            arrived(column_t if text else column_i, place, c_recv.at[q])

    rows = []
    for k in range(2):
        v = column_t[k].astype(f32)
        rows.append(jnp.concatenate([v[0:8], v[8:16]], axis=1))
    bundle[0:16, :] = jnp.concatenate(rows, axis=0).astype(bf16)
    rows = []
    for k in range(6):
        v = column_i[k].astype(f32)
        rows.append(jnp.concatenate([v[2 * p : 2 * p + 2] for p in range(5)], axis=1))
    rows.append(jnp.zeros((4, KEYED), f32))
    bundle[16:32, :] = jnp.concatenate(rows, axis=0).astype(bf16)

    for d in range(1, N_Y):
        copy = pltpu.make_async_remote_copy(
            src_ref=bundle, dst_ref=others.at[d], send_sem=o_send.at[d], recv_sem=o_recv.at[d],
            device_id=far_to(d), device_id_type=MESH,
        )
        copy.start()
        pending.append(copy)

    def straight():
        return pltpu.make_async_remote_copy(
            src_ref=bundle, dst_ref=others.at[0], send_sem=o_send.at[0], recv_sem=o_recv.at[0],
            device_id=far_to(0), device_id_type=MESH,
        )

    @pl.when(role != 0)
    def _():
        copy = straight()
        copy.start()
        copy.wait()

    @pl.when(role == 0)
    def _():
        others[0] = bundle[...]

    for d in range(1, N_Y):
        arrived(others, d, o_recv.at[d])

    scale = scale_ref[0]
    bias = bias_ref[0]
    far = others[...].reshape(N_Y * 32, KEYED)
    logits = scale * dot_nt(bundle[:, :D], far[:, :D]) + bias
    lane = lax.broadcasted_iota(jnp.int32, (32, LANES), 1)
    place = lax.broadcasted_iota(jnp.int32, (32, LANES), 0)
    base = jnp.where(lane == 0, 16.0, jnp.where(lane == 1, 1.0, 0.0)).astype(bf16)
    key_col = dot_nt(base, far[:, D:])
    key_row = dot_nt(bundle[:, D:], jnp.concatenate([base] * 4, axis=0))
    lane32 = lax.rem(lane, 32)
    row_text, col_text = place < 16, lane32 < 16
    row_image = jnp.logical_and(place >= 16, place < 28)
    col_image = jnp.logical_and(lane32 >= 16, lane32 < 28)
    cross = jnp.logical_or(
        jnp.logical_and(row_text, col_image), jnp.logical_and(row_image, col_text)
    )
    match = jnp.where(key_col == key_row, 1.0, 0.0)
    coef = jnp.where(cross, loss_scale * (jax.nn.sigmoid(logits) - match), 0.0).astype(bf16)
    share = scale * dot_nn(coef, far[:, :D])
    third = D // 3
    for k in range(2):
        part_t[k] = share[8 * k : 8 * k + 8]
    for k in range(6):
        v = share[16 + 2 * k : 18 + 2 * k]
        v = [v[:, p * third : (p + 1) * third] for p in range(3)] + [jnp.zeros((2, third), f32)]
        part_i[k] = jnp.concatenate(v, axis=0)

    def to_owner(q):
        text, place = place_of(q)
        src, dst = (part_t, gsum_t) if text else (part_i, gsum_i)
        return pltpu.make_async_remote_copy(
            src_ref=src.at[place], dst_ref=dst.at[role], send_sem=g_send.at[q], recv_sem=g_recv.at[role],
            device_id=device_of(q // 2, y, z, q % 2), device_id_type=MESH,
        )

    for q in range(8):

        @pl.when(role != q)
        def _():
            to_owner(q).start()

    @pl.when(is_text)
    def _():
        gsum_t[role] = part_t[x_lo]
        for d in range(1, 8):
            q = lax.rem(role + d, 8)
            arrived(gsum_t, q, g_recv.at[q])
        v = gsum_t[0]
        for q in range(1, 8):
            v = v + gsum_t[q]
        grad_at[...] = v

    @pl.when(jnp.logical_not(is_text))
    def _():
        gsum_i[role] = part_i[x_lo * 3 + tower]
        for d in range(1, 8):
            q = lax.rem(role + d, 8)
            arrived(gsum_i, q, g_recv.at[q])
        v = gsum_i[0]
        for q in range(1, 8):
            v = v + gsum_i[q]
        v = jnp.concatenate([v[2 * p : 2 * p + 2] for p in range(3)], axis=1)
        grad_at[...] = jnp.where(seg < 4, v[0:1], v[1:2])

    grad = grad_at[...]
    grad = (grad - unit * jnp.sum(unit * grad, axis=-1, keepdims=True)) / norm
    grad = grad / count
    grad_rows = grad.astype(bf16)

    def back(width, weights, slope_of, at):
        gh = dot_nt(grad_rows, weights)
        for j in range(8):
            rows = slice(j * SEG, (j + 1) * SEG)
            gpre[rows, at : at + width] = (slope_of(rows) * gh[j : j + 1, :]).astype(bf16)

    for g in range(8):
        back(GROUP, wb[g].reshape(GROUP, D), lambda rows, g=g: slope[g, rows, :], g * GROUP)
    back(LANES, eb[...].reshape(LANES, D), lambda rows: slope_e[rows, :], 8 * GROUP)
    out_ref[...] = dot_nn(gpre[:, : 8 * GROUP], wa[...].reshape(8 * GROUP, D)) + dot_nn(
        gpre[:, 8 * GROUP :], ea[...].reshape(LANES, D)
    )
    for j in range(8):
        rows = slice(j * SEG, (j + 1) * SEG)
        standard, inv_std = normalise(x_ref[rows, :])
        grad_std = out_ref[rows, :] * gain
        m1 = jnp.mean(grad_std, axis=-1, keepdims=True)
        m2 = jnp.mean(grad_std * standard, axis=-1, keepdims=True)
        out_ref[rows, :] = grad[j : j + 1, :] * mask_of(rows, D) + inv_std * (
            grad_std - m1 - standard * m2
        )
        pltpu.make_async_copy(out_ref.at[rows], out_hbm.at[rows], out_sem.at[j]).start()
    for j in range(8):
        rows = slice(j * SEG, (j + 1) * SEG)
        pltpu.make_async_copy(out_ref.at[rows], out_hbm.at[rows], out_sem.at[j]).wait()
    for copy in pending:
        copy.wait_send()

    @pl.when(is_text)
    def _():
        for d in range(1, 8):
            to_column(True, d).wait_send()

    @pl.when(jnp.logical_not(is_text))
    def _():
        for d in range(1, 8):
            to_column(False, d).wait_send()

    for q in range(8):

        @pl.when(role != q)
        def _():
            to_owner(q).wait_send()


def body(layer_input, caption_ids, positives, ln_gain, w_first, w_second, logit_scale, logit_bias):
    anywhere = pl.BlockSpec(memory_space=pl.ANY)
    smem = pl.BlockSpec(memory_space=pltpu.SMEM)
    dma = pltpu.SemaphoreType.DMA
    return pl.pallas_call(
        kernel,
        out_shape=jax.ShapeDtypeStruct((ROWS, D), f32),
        in_specs=[anywhere] * 5 + [smem] * 3,
        out_specs=anywhere,
        scratch_shapes=[
            pltpu.VMEM((ROWS, D), bf16),
            pltpu.VMEM((8, SEG), jnp.int32),
            pltpu.VMEM((2, D), f32),
            pltpu.VMEM((34, 2, D), bf16),
            pltpu.VMEM((34, 2, D), bf16),
            pltpu.VMEM((ROWS, D), f32),
            dma((5,)),
            dma((8,)),
            pltpu.VMEM((8, N_Z, MAIN, D), bf16),
            pltpu.VMEM((8, N_Z, MAIN, D), bf16),
            pltpu.VMEM((8, EXTRA, D), bf16),
            pltpu.VMEM((8, EXTRA, D), bf16),
            pltpu.VMEM((6, EXTRA, D), bf16),
            pltpu.VMEM((6, EXTRA, D), bf16),
            pltpu.VMEM((ROWS, D), bf16),
            pltpu.VMEM((ROWS, GROUP), f32),
            pltpu.VMEM((8, ROWS, GROUP), f32),
            pltpu.VMEM((ROWS, LANES), f32),
            pltpu.VMEM((8, 8, GROUP), f32),
            pltpu.VMEM((8, LANES), f32),
            pltpu.VMEM((16, D), f32),
            pltpu.VMEM((8, ROWS), bf16),
            pltpu.VMEM((ROWS, LANES), f32),
            pltpu.VMEM((16, KEYED // 2), bf16),
            pltpu.VMEM((16, KEYED // 5), bf16),
            pltpu.VMEM((2, 16, KEYED // 2), bf16),
            pltpu.VMEM((6, 16, KEYED // 5), bf16),
            pltpu.VMEM((32, KEYED), bf16),
            pltpu.VMEM((N_Y, 32, KEYED), bf16),
            pltpu.VMEM((2, 8, D), f32),
            pltpu.VMEM((6, 8, D // 3), f32),
            pltpu.VMEM((8, 8, D), f32),
            pltpu.VMEM((8, 8, D // 3), f32),
            pltpu.VMEM((8, D), f32),
            pltpu.VMEM((ROWS, 8 * GROUP + LANES), bf16),
            dma((2, 8, 8)),
            dma((2, 4)),
            dma((2,)),
            dma((2, 2, 8)),
            dma((2, 3)),
            dma((2,)),
            dma((2, 2, 4)),
            dma((2, 2, 3)),
            dma((2, 3)),
            dma((2, 8)),
            dma((2, 7)),
            dma((2, 3)),
            dma((2, 3, 8)),
            dma((2, 3)),
            dma((2, 4, 8)),
            dma((2, 4)),
            dma((7,)),
            dma((8,)),
            dma((4,)),
            dma((4,)),
            dma((8,)),
            dma((8,)),
        ],
        compiler_params=pltpu.CompilerParams(
            collective_id=0, has_side_effects=True, vmem_limit_bytes=56 * 2**20
        ),
        name="step",
    )(
        layer_input, caption_ids, ln_gain, jnp.transpose(w_first, (2, 0, 1)), jnp.transpose(w_second, (1, 0, 2)),
        positives, logit_scale, logit_bias,
    )


def solution(mesh):
    placed = (
        P(("blk", "tower"), None),
        P("blk", None),
        P("blk"),
        P(),
        P(None, None, "blk"),
        P(None, "blk", None),
        P(),
        P(),
    )
    return jax.shard_map(
        body, mesh=mesh, in_specs=placed, out_specs=P(("blk", "tower"), None), check_vma=False
    )
```
